32 devices in a mesh: groups: 2 (over x), tiles: 16 (over z, y, core).
Axes of the slice: x: 2, y: 2, z: 4, core: 2. Of those that a mesh axis runs over, the one named last changes fastest.
Arguments:
- warmth_deviation: float32 [512, 32, 128], P(('groups', 'tiles')), parts along dimension 0, may hold values from -6 to 6
- brine_deviation: float32 [512, 32, 128], P(('groups', 'tiles')), parts along dimension 0, may hold values from -6 to 6
- marine_flag_grid: int32 [512, 32], P(('groups', 'tiles')), parts along dimension 0, may hold values 0 or 1
- flooded_tier_tally: int32 [512, 32], P(('groups', 'tiles')), parts along dimension 0, may hold values from 1 to 75
- assigned_trainer: int32 [512, 32], P(('groups', 'tiles')), parts along dimension 0, may hold values from 0 to 15, as said below
- desired_spreading_rates: bfloat16 [512, 32, 128], P(('groups', 'tiles')), parts along dimension 0, may hold values from -3 to 3
- leading_intercepts: float32 [32, 1024], P(('groups', 'tiles')), parts along dimension 0, may hold values from -3 to 3
- leading_map_values: bfloat16 [256, 1024], replicated, may hold values from -0.75 to 0.75
- interior_maps: bfloat16 [2, 1024, 1024], replicated, may hold values from -0.25 to 0.25
- readout_map_values: bfloat16 [1024, 128], replicated, may hold values from -0.25 to 0.25
Outputs:
- stepped_water_state: float32 [2, 512, 32, 128], P(None, ('groups', 'tiles')), parts along dimension 1
- inferred_spreading_rates: bfloat16 [512, 32, 128], P(('groups', 'tiles')), parts along dimension 0
- leading_grad_values: float32 [512, 1024], P('groups'), parts along dimension 0
- interior_grad_values: float32 [2, 2048, 1024], P(None, 'groups'), parts along dimension 1
- readout_grad_values: float32 [2048, 128], P('groups'), parts along dimension 0
- intercept_grad_values: float32 [32, 1024], P(('groups', 'tiles')), parts along dimension 0
The draws below stay inside these ranges and needn't reach their ends.
There are 2 independent parts, one for each index of `groups`. The reference program is written for one: setup_inputs(seed, part) draws one part's arguments, and reference() takes and returns one part's arrays. A program takes and returns all parts, laid end to end along the dimension named above; an argument that names none is the same for every part. Nothing has to cross between parts.
Inputs may be any that keep to these rules, and one draw needn't show every extreme that they name: `assigned_trainer`: each tile has at most 64 columns assigned to one learner; in every draw one learner receives exactly 64 columns from every tile.
All inputs are finite; a program needn't handle non-finite values. No bound on the sum of `marine_flag_grid` on one device may be relied on, other than what follows from the above.
Results may differ from the reference program's by a relative error of at most 0.012.
Values may be sent and summed in bfloat16 or wider, within the bound.
No kernel may reach another device: no remote copies, remote signals or barrier semaphores. Data moves between devices by JAX's collectives and lax.ppermute only.
A program may use at most 128 MiB of HBM per device.

```python
import math
import jax
import jax.numpy as jnp
from jax import lax

LON_DEV = 16
NORTH_SOUTH_BAND = 32
LEVELS = 75
STRATUM_GROUPING = 128
HID = 1024
DEEP = 2
FEAT = 256
LEARNERS = 16
EAST_WEST_EXTENT = 256


def draw_assigned_trainer(key, part):
    key = jax.random.fold_in(key, 7)
    student_models = EAST_WEST_EXTENT // LON_DEV
    upright_piles = LON_DEV * NORTH_SOUTH_BAND
    room_limit = 2 * upright_piles // student_models
    busiest = jax.random.randint(jax.random.fold_in(key, 1), (), 0, student_models)
    spare_slots = (busiest + 1 + jnp.arange((student_models - 1) * room_limit, dtype=jnp.int32) // room_limit) % student_models

    def one_tile(tile_key):
        first_key, second_key = jax.random.split(tile_key)
        picked = jax.random.permutation(first_key, spare_slots)[:upright_piles - room_limit]
        chosen = jnp.concatenate([jnp.zeros((room_limit,), jnp.int32) + busiest, picked.astype(jnp.int32)])
        return jax.random.permutation(second_key, chosen).reshape(LON_DEV, NORTH_SOUTH_BAND)
    tile_keys = jax.random.split(jax.random.fold_in(key, 2), student_models)
    return jax.vmap(one_tile)(tile_keys).reshape(EAST_WEST_EXTENT, NORTH_SOUTH_BAND).astype(jnp.int32)


def touch_ends(values, own_key, smallest, high):
    shape = values.shape
    place = [jax.random.randint(jax.random.fold_in(own_key, axis), (), 0, shape[axis]) for axis in range(len(shape))]
    values = values.at[tuple(place)].set(smallest)
    longest = shape.index(max(shape))
    place[longest] = (place[longest] + 1) % shape[longest]
    return values.at[tuple(place)].set(high)


def shard_levels(own_key, extent, pieces, low, largest):
    gain, own = 1.0, jax.random.fold_in(own_key, 6)
    for dim, shards_of in pieces:
        heights = jnp.exp(jax.random.uniform(jax.random.fold_in(own, dim), (shards_of,), jnp.float32, low / len(pieces), largest / len(pieces)))
        gain = gain * jnp.repeat(heights, extent[dim] // shards_of).reshape([-1 if axis == dim else 1 for axis in range(len(extent))])
    return gain


def gaussian(own_key, dims, deviation, most, pieces=(), kind=jnp.bfloat16):
    gain = shard_levels(own_key, dims, pieces, -0.22, 0.18) if pieces else 1.0
    entries = jax.random.normal(own_key, dims, jnp.float32) * deviation * gain
    return jnp.minimum(jnp.maximum(entries, -most), most).astype(kind)


def setup_inputs(seed: int = 0, part: int = 0) -> dict:
    streams_of = jax.random.split(jax.random.key(seed), 11)
    own_keys = jax.random.split(jax.random.fold_in(streams_of[10], part), 11)
    return {
        "warmth_deviation": gaussian(own_keys[0], (EAST_WEST_EXTENT, NORTH_SOUTH_BAND, STRATUM_GROUPING), 1.0, 6.0, ((0, 16),), jnp.float32),
        "brine_deviation": gaussian(own_keys[1], (EAST_WEST_EXTENT, NORTH_SOUTH_BAND, STRATUM_GROUPING), 1.0, 6.0, ((0, 16),), jnp.float32),
        "marine_flag_grid": touch_ends((jax.random.randint(own_keys[2], (EAST_WEST_EXTENT, NORTH_SOUTH_BAND), 0, 4) < 3).astype(jnp.int32), jax.random.fold_in(own_keys[2], 1), 0, 1),
        "flooded_tier_tally": touch_ends(jax.random.randint(own_keys[3], (EAST_WEST_EXTENT, NORTH_SOUTH_BAND), 1, LEVELS + 1), jax.random.fold_in(own_keys[3], 1), 1, LEVELS).astype(jnp.int32),
        "assigned_trainer": draw_assigned_trainer(jax.random.fold_in(jax.random.fold_in(streams_of[10], part), 71), part),
        "desired_spreading_rates": gaussian(own_keys[5], (EAST_WEST_EXTENT, NORTH_SOUTH_BAND, STRATUM_GROUPING), 0.5, 3.0, ((0, 16),)),
        "leading_intercepts": gaussian(own_keys[6], (LEARNERS, HID), 0.5, 3.0, ((0, 16),), jnp.float32),
        "leading_map_values": gaussian(streams_of[7], (FEAT, HID), LEVELS ** -0.5, 0.75),
        "interior_maps": gaussian(streams_of[8], (DEEP, HID, HID), (HID // 2) ** -0.5, 0.25),
        "readout_map_values": gaussian(streams_of[9], (HID, STRATUM_GROUPING), (HID // 2) ** -0.5, 0.25),
    }


KAPPA = 0.2

def silu_slope(pre_act):
    logistic = jax.nn.sigmoid(pre_act)
    return logistic * (1.0 + pre_act * (1.0 - logistic))

def contract_rows(left_rows, right_rows):
    return lax.dot_general(left_rows, right_rows, (((0,), (0,)), ((), ())), preferred_element_type=jnp.float32)

def times_transposed(left_rows, right_rows):
    return lax.dot_general(left_rows, right_rows, (((1,), (1,)), ((), ())), preferred_element_type=jnp.float32)

def wet_levels(marine_flag_grid, flooded_tier_tally, water_stratification):
    level_index = jnp.arange(water_stratification, dtype=jnp.int32)
    return ((level_index < flooded_tier_tally[..., None]) & (marine_flag_grid[..., None] > 0)).astype(jnp.float32)

def spread_apart(bordered_with_ghosts):
    padded = jnp.pad(bordered_with_ghosts, ((0, 0), (0, 0), (1, 1), (0, 0)))
    centre = padded[:, 1:-1, 1:-1]
    summed = jnp.zeros_like(centre[:2])
    for beside in (padded[:, 2:, 1:-1], padded[:, :-2, 1:-1], padded[:, 1:-1, 2:], padded[:, 1:-1, :-2]):
        summed = summed + beside[2] * (beside[:2] - centre[:2])
    return centre[:2] + KAPPA * centre[2] * summed

def train_rows(descriptor_values, bias_rows, targets, wet_rows, leading_map_values, interior_maps, readout_map_values, loss_scale):
    pre_act = jnp.dot(descriptor_values, leading_map_values, preferred_element_type=jnp.float32) + bias_rows
    pre_list = [pre_act]
    active = jax.nn.silu(pre_act).astype(jnp.bfloat16)
    active_list = [active]
    for layer_index in range(interior_maps.shape[0]):
        pre_act = jnp.dot(active, interior_maps[layer_index], preferred_element_type=jnp.float32)
        pre_list.append(pre_act)
        active = jax.nn.silu(pre_act).astype(jnp.bfloat16)
        active_list.append(active)
    output = jnp.dot(active, readout_map_values, preferred_element_type=jnp.float32)
    residual_rows = ((output - targets.astype(jnp.float32)) * wet_rows * loss_scale).astype(jnp.bfloat16)
    readout_grad_values = contract_rows(active, residual_rows)
    upward = times_transposed(residual_rows, readout_map_values)
    grad_layers = []
    for layer_index in reversed(range(interior_maps.shape[0])):
        error_signals = (upward * silu_slope(pre_list[layer_index + 1])).astype(jnp.bfloat16)
        grad_layers.insert(0, contract_rows(active_list[layer_index], error_signals))
        upward = times_transposed(error_signals, interior_maps[layer_index])
    error_signals = (upward * silu_slope(pre_list[0])).astype(jnp.bfloat16)
    leading_grad_values = contract_rows(descriptor_values, error_signals)
    return (output.astype(jnp.bfloat16), error_signals, leading_grad_values, jnp.stack(grad_layers), readout_grad_values)

def reference(warmth_deviation, brine_deviation, marine_flag_grid, flooded_tier_tally, assigned_trainer, desired_spreading_rates, leading_intercepts, leading_map_values, interior_maps, readout_map_values):
    water_stratification = warmth_deviation.shape[-1]
    upright_piles = warmth_deviation.shape[0] * warmth_deviation.shape[1]
    marine_locations = wet_levels(marine_flag_grid, flooded_tier_tally, water_stratification)
    carried_fluid_state = jnp.stack([warmth_deviation, brine_deviation, marine_locations])
    bordered_with_ghosts = jnp.concatenate([carried_fluid_state[:, -1:], carried_fluid_state, carried_fluid_state[:, :1]], axis=1)
    stepped_water_state = spread_apart(bordered_with_ghosts)
    descriptor_values = (stepped_water_state * marine_locations).transpose(1, 2, 0, 3).reshape(upright_piles, 2 * water_stratification).astype(jnp.bfloat16)
    flat_assign = assigned_trainer.reshape(upright_piles).astype(jnp.int32)
    bias_rows = leading_intercepts[flat_assign]
    loss_scale = 1.0 / math.sqrt(upright_piles)
    outcomes = train_rows(descriptor_values, bias_rows, desired_spreading_rates.reshape(upright_piles, water_stratification), marine_locations.reshape(upright_piles, water_stratification), leading_map_values, interior_maps, readout_map_values, loss_scale)
    inferred_stirring_rate, error_signals, leading_grad_values, interior_grad_values, readout_grad_values = outcomes
    selector = (flat_assign[:, None] == jnp.arange(leading_intercepts.shape[0], dtype=jnp.int32)[None, :]).astype(jnp.bfloat16)
    intercept_grad_values = contract_rows(selector, error_signals)
    return (stepped_water_state, inferred_stirring_rate.reshape(warmth_deviation.shape), leading_grad_values, interior_grad_values, readout_grad_values, intercept_grad_values)
```

```python
import math

import jax
import jax.numpy as jnp
from jax import lax
from jax.sharding import PartitionSpec as P

KAPPA = 0.2
LEVELS = 75
KEPT = 80
BF = jnp.bfloat16
F32 = jnp.float32


def contract_rows(left, right):
    return lax.dot_general(left, right, (((0,), (0,)), ((), ())), preferred_element_type=F32)


def times_transposed(left, right):
    return lax.dot_general(left, right, (((1,), (1,)), ((), ())), preferred_element_type=F32)


def silu_slope(pre):
    s = jax.nn.sigmoid(pre)
    return s * (1.0 + pre * (1.0 - s))


def add(a, b):
    return (a.astype(F32) + b.astype(F32)).astype(BF)


def swap(x, stride):
    n = lax.axis_size("tiles")
    return lax.ppermute(x, "tiles", [(t, t ^ stride) for t in range(n)])


def bit_of(stride):
    return (lax.axis_index("tiles") // stride) % 2


def halve(x, stride):
    bit = bit_of(stride)
    parts = x.reshape(2, x.shape[0] // 2, x.shape[1])
    mine = lax.dynamic_index_in_dim(parts, bit, 0, False)
    other = lax.dynamic_index_in_dim(parts, 1 - bit, 0, False)
    return add(mine, swap(other, stride))


def join(x, stride):
    bit = bit_of(stride)
    got = swap(x, stride)
    return jnp.concatenate([jnp.where(bit == 0, x, got), jnp.where(bit == 0, got, x)], 0)


def reduce_tiles(x):
    n = lax.axis_size("tiles")
    x = halve(x, 1)
    rows = x.shape[0] // 2
    a, b = x[:rows], x[rows:]
    a, b = halve(a, 2), halve(b, 4)
    a, b = halve(a, 4), halve(b, 2)
    m = jnp.concatenate([a, b], 0)
    stride = 8
    while stride < n:
        m = add(m, swap(m, stride))
        stride *= 2
    rows = a.shape[0]
    a, b = m[:rows], m[rows:]
    a, b = join(a, 4), join(b, 2)
    a, b = join(a, 2), join(b, 4)
    return join(jnp.concatenate([a, b], 0), 1)


def local(
    warmth,
    brine,
    flags,
    tally,
    assigned,
    desired,
    intercepts,
    leading,
    interior,
    readout,
):
    n = lax.axis_size("tiles")
    lon, lat, levels = warmth.shape
    cols = lon * lat
    hid = leading.shape[1]
    scale = 1.0 / math.sqrt(cols * n)

    up = [(i, (i + 1) % n) for i in range(n)]
    down = [(j, i) for i, j in up]
    depth = jnp.where(flags > 0, tally, 0)
    depth_plane = jnp.broadcast_to(depth[:, :, None].astype(F32), (lon, lat, levels))
    state = jnp.stack([warmth, brine, depth_plane])
    before = lax.ppermute(state[:, -1:], "tiles", up)
    after = lax.ppermute(state[:, :1], "tiles", down)
    bias = lax.all_to_all(
        jnp.broadcast_to(intercepts, (n, hid)), "tiles", split_axis=0, concat_axis=0, tiled=True
    )
    level = lax.broadcasted_iota(jnp.int32, (1, 1, 1, levels), 3).astype(F32)
    wide = jnp.concatenate([before, state, after], 1)
    wet = (level[0] < wide[2]).astype(F32)
    q = wide[:2]
    centre = q[:, 1:-1]
    wet_c = wet[1:-1]
    zrow = jnp.zeros((lon, 1, levels), F32)
    zq = jnp.zeros((2, lon, 1, levels), F32)
    total = wet[2:] * (q[:, 2:] - centre)
    total = total + wet[:-2] * (q[:, :-2] - centre)
    total = total + jnp.concatenate([wet_c[:, 1:], zrow], 1) * (
        jnp.concatenate([centre[:, :, 1:], zq], 2) - centre
    )
    total = total + jnp.concatenate([zrow, wet_c[:, :-1]], 1) * (
        jnp.concatenate([zq, centre[:, :, :-1]], 2) - centre
    )
    stepped = centre + KAPPA * wet_c * total

    wet_rows = wet_c.reshape(cols, levels)
    lane = lax.broadcasted_iota(jnp.int32, (cols, levels), 1)
    own = lane == assigned.reshape(cols, 1) + KEPT
    feats = [
        jnp.where(own, 1.0, stepped[i].reshape(cols, levels) * wet_rows).astype(BF)
        for i in range(2)
    ]
    features = jnp.concatenate(feats, 1)
    bias_hi = bias.astype(BF)
    bias_lo = (bias - bias_hi.astype(F32)).astype(BF)
    first = jnp.concatenate(
        [
            leading[:KEPT],
            bias_hi,
            leading[KEPT + n : levels + KEPT],
            bias_lo,
            leading[levels + KEPT + n :],
        ],
        0,
    )

    pres = [jnp.dot(features, first, preferred_element_type=F32)]
    acts = [jax.nn.silu(pres[0]).astype(BF)]
    deep = interior.shape[0]
    for i in range(deep):
        pres.append(jnp.dot(acts[-1], interior[i], preferred_element_type=F32))
        acts.append(jax.nn.silu(pres[-1]).astype(BF))
    output = jnp.dot(acts[-1], readout, preferred_element_type=F32)
    err = (
        (output - desired.reshape(cols, levels).astype(F32)) * wet_rows * scale
    ).astype(BF)
    readout_t = contract_rows(err, acts[-1]).astype(BF)[:KEPT]
    back = times_transposed(err, readout)
    grads = [None] * deep
    for i in reversed(range(deep)):
        delta = (back * silu_slope(pres[i + 1])).astype(BF)
        grads[i] = contract_rows(acts[i], delta).astype(BF)
        if i > 0:
            grads[i] = reduce_tiles(grads[i])
        back = times_transposed(delta, interior[i])
    delta = (back * silu_slope(pres[0])).astype(BF)
    lead = contract_rows(features, delta).astype(BF)
    split = KEPT + n
    pad = (-(split + 2 * KEPT)) % 256
    last = jnp.concatenate(
        [
            grads[0],
            lead[:split],
            lead[levels : levels + KEPT],
            readout_t,
            jnp.zeros((pad, hid), BF),
        ],
        0,
    )
    last = reduce_tiles(last)
    grads[0] = last[:hid]
    low, mid, high = hid + KEPT, hid + split, hid + split + KEPT
    zeros = jnp.zeros((levels - KEPT, hid), F32)
    lead_out = jnp.concatenate(
        [last[hid:low].astype(F32), zeros, last[mid:high].astype(F32), zeros], 0
    )
    readout_out = jnp.pad(
        last[high : high + KEPT].astype(F32).T, ((0, 0), (0, levels - KEPT))
    )
    intercept_out = lax.dynamic_slice_in_dim(
        last, low + lax.axis_index("tiles"), 1, 0
    ).astype(F32)
    return (
        stepped,
        output.astype(BF).reshape(lon, lat, levels),
        lead_out,
        jnp.stack([g.astype(F32) for g in grads]),
        readout_out,
        intercept_out,
    )


def solution(mesh):
    part = ("groups", "tiles")
    return jax.shard_map(
        local,
        mesh=mesh,
        in_specs=(
            P(part, None, None),
            P(part, None, None),
            P(part, None),
            P(part, None),
            P(part, None),
            P(part, None, None),
            P(part, None),
            P(),
            P(),
            P(),
        ),
        out_specs=(
            P(None, part, None, None),
            P(part, None, None),
            P("groups", None),
            P(None, "groups", None),
            P("groups", None),
            P(part, None),
        ),
        check_vma=False,
    )
```

```python
import functools
import math

import jax
import jax.numpy as jnp
from jax import lax
from jax.experimental import pallas as pl
from jax.experimental.pallas import tpu as pltpu
from jax.sharding import PartitionSpec as P

KAPPA = 0.2
KEPT = 80
BLOCK = 256
TOP_SHARE = 0.5
ROOM = 44
LOW_SHARE = 0.6
BF = jnp.bfloat16
F32 = jnp.float32
VMEM = pl.BlockSpec(memory_space=pltpu.VMEM)
ANY = pl.BlockSpec(memory_space=pl.ANY)
HBM = pl.BlockSpec(memory_space=pltpu.HBM)
Shape = jax.ShapeDtypeStruct


def contract_rows(left, right):
    return lax.dot_general(left, right, (((0,), (0,)), ((), ())), preferred_element_type=F32)


def times_transposed(left, right):
    return lax.dot_general(left, right, (((1,), (1,)), ((), ())), preferred_element_type=F32)


def bit_of(stride):
    return (lax.axis_index("tiles") // stride) % 2


def rows_at(index, rows):
    return pl.ds(pl.multiple_of(index * rows, rows), rows)


def rest_rows(n):
    return -(-(n + 3 * KEPT) // 256) * 256


def call(
    body, outs, args, after=None, carry=(), specs=None, out_specs=None, scratch=(), aliases=None, room=12
):
    outs, args = tuple(outs), tuple(args)
    specs = list(specs or [VMEM] * len(args))
    out_specs = list(out_specs or [VMEM] * len(outs))
    count, made = len(args), len(outs)
    aliases = dict(aliases or {})
    extra = (() if after is None else (after,)) + tuple(carry)
    for i, array in enumerate(carry):
        aliases[count + len(extra) - len(carry) + i] = made + i
    plain = body

    def body(*refs):
        given = refs[:count]
        rest = refs[count + len(extra) :]
        plain(*given, *rest[:made], *rest[made + len(carry) :])

    return pl.pallas_call(
        body,
        out_shape=outs + tuple(Shape(a.shape, a.dtype) for a in carry),
        in_specs=specs + [ANY] * len(extra),
        out_specs=tuple(out_specs + [ANY] * len(carry)),
        scratch_shapes=scratch,
        input_output_aliases=aliases,
        compiler_params=pltpu.CompilerParams(vmem_limit_bytes=room * 2**20),
        cost_estimate=pl.CostEstimate(flops=1, bytes_accessed=1, transcendentals=0),
    )(*args, *extra)


def activate(v):
    s = 0.5 + 0.5 * jnp.tanh(0.5 * v)
    act = v * s
    return act.astype(BF), (s + act * (1.0 - s)).astype(BF)


def step_body(depth, before, after, owner, warm, brine, stepped, feat, wet_out):
    lon, lat, levels = warm.shape
    cols = lon * lat
    level = lax.broadcasted_iota(jnp.int32, (lon, lat, levels), 2).astype(F32)
    row = lax.broadcasted_iota(jnp.int32, (lon, lat, levels), 1)
    wet = (level < depth[...]).astype(F32)
    wet_b = (level[:1] < before[2]).astype(F32)
    wet_a = (level[:1] < after[2]).astype(F32)
    wet_e = jnp.concatenate([wet[1:], wet_a], 0)
    wet_w = jnp.concatenate([wet_b, wet[:-1]], 0)
    wet_n = jnp.where(row < lat - 1, pltpu.roll(wet, lat - 1, 1), 0.0)
    wet_s = jnp.where(row > 0, pltpu.roll(wet, 1, 1), 0.0)
    wet_out[...] = wet.reshape(cols, levels)
    lane = lax.broadcasted_iota(jnp.int32, (cols, levels), 1)
    own = lane == owner[...].reshape(cols, levels)
    for i, ref in enumerate((warm, brine)):
        q = ref[...]
        total = wet_e * (jnp.concatenate([q[1:], after[i]], 0) - q)
        total = total + wet_w * (jnp.concatenate([before[i], q[:-1]], 0) - q)
        total = total + wet_n * (pltpu.roll(q, lat - 1, 1) - q)
        total = total + wet_s * (pltpu.roll(q, 1, 1) - q)
        out = q + KAPPA * wet * total
        stepped[i] = out
        feat[:, i * levels : (i + 1) * levels] = jnp.where(
            own, 1.0, (out * wet).reshape(cols, levels)
        ).astype(BF)


def weight_grad(act, delta, half, out, rows):
    for j in range(0, rows, BLOCK):
        at = pl.ds(pl.multiple_of(half * rows + j, BLOCK), BLOCK)
        out[j : j + BLOCK] = contract_rows(act[:, at], delta[...]).astype(BF)


def back_through(delta, weights, slope, out):
    for j in range(0, out.shape[1], BLOCK):
        back = times_transposed(delta, weights[j : j + BLOCK])
        out[:, j : j + BLOCK] = (back * slope[:, j : j + BLOCK].astype(F32)).astype(BF)


def forward_body(
    n,
    scale,
    feat,
    wet,
    bias,
    desired,
    leading,
    interior,
    readout,
    inferred,
    act0,
    act1,
    slope0,
    slope1,
    delta2,
    other,
    rest,
    w_lead,
    w_int,
    act2,
    slope2,
    sems,
):
    cols, levels = wet.shape
    hid = readout.shape[0]
    copies = [
        pltpu.make_async_copy(interior.at[i], w_int.at[i], sems.at[i])
        for i in range(interior.shape[0])
    ]
    for copy in copies:
        copy.start()
    w_lead[...] = leading[...]
    for j in range(bias.shape[1]):
        value = bias[:, j]
        high = value.astype(BF)
        at = slice(j * bias.shape[2], (j + 1) * bias.shape[2])
        w_lead[KEPT : KEPT + n, at] = high
        w_lead[levels + KEPT : levels + KEPT + n, at] = (value - high.astype(F32)).astype(BF)
    for layer, (left, right, act, slope) in enumerate(
        (
            (feat, w_lead, act0, slope0),
            (act0, w_int.at[0], act1, slope1),
            (act1, w_int.at[1], act2, slope2),
        )
    ):
        if layer:
            copies[layer - 1].wait()
        for j in range(0, hid, BLOCK):
            pre = jnp.dot(left[...], right[:, j : j + BLOCK], preferred_element_type=F32)
            act[:, j : j + BLOCK], slope[:, j : j + BLOCK] = activate(pre)
    output = jnp.dot(act2[...], readout[...], preferred_element_type=F32)
    inferred[...] = output.astype(BF).reshape(inferred.shape)
    target = desired[...].reshape(cols, levels).astype(F32)
    err = ((output - target) * wet[...] * scale).astype(BF)
    back_through(err, readout, slope2, delta2)
    weight_grad(act1, delta2, 1 - bit_of(1), other, hid // 2)
    rest[...] = contract_rows(err, act2[...]).astype(BF)[:KEPT]


def middle_body(
    interior, act0, act1, slope1, delta2, mine, delta1, below_other, w_int, sems
):
    hid = act0.shape[1]
    copy = pltpu.make_async_copy(interior.at[1], w_int, sems.at[0])
    copy.start()
    bit = bit_of(1)
    weight_grad(act1, delta2, bit, mine, hid // 2)
    copy.wait()
    back_through(delta2[...], w_int, slope1, delta1)
    weight_grad(act0, delta1, 1 - bit, below_other, hid // 2)


def first_body(
    n,
    interior,
    feat,
    act0,
    slope0,
    delta1,
    readout_in,
    other_in,
    mine,
    other,
    delta0,
    rest,
    w_int,
    sems,
):
    levels = feat.shape[1] // 2
    hid = slope0.shape[1]
    half = hid // 2
    copy = pltpu.make_async_copy(interior.at[0], w_int, sems.at[0])
    copy.start()
    bit = bit_of(1)
    other[:half] = other_in[...]
    weight_grad(act0, delta1, bit, mine, half)
    copy.wait()
    back_through(delta1[...], w_int, slope0, delta0)
    lead = contract_rows(feat[...], delta0[...]).astype(BF)
    a = KEPT + n
    rest[:a] = lead[:a]
    rest[a : a + KEPT] = lead[levels : levels + KEPT]
    rest[a + KEPT : a + 2 * KEPT] = readout_in[...]
    rows = rest.shape[0]
    if rows > a + 2 * KEPT:
        rest[a + 2 * KEPT :] = jnp.zeros((rows - a - 2 * KEPT, hid), BF)
    for ref, b in ((other, 1 - bit), (mine, bit)):
        ref[half:] = rest[rows_at(b, rows // 2)]


def split_body(mine, got, a_mine, a_other, b_mine, b_other):
    base = 0
    for stride, keep, send in ((2, a_mine, a_other), (4, b_mine, b_other)):
        bit = bit_of(stride)
        rows = keep.shape[0]
        for ref, b in ((send, 1 - bit), (keep, bit)):
            at = pl.ds(pl.multiple_of(base + b * rows, 16), rows)
            ref[...] = mine[at] + got[at]
        base += 2 * rows


def halve_body(a, got_a, b, got_b, a_mine, a_other, b_mine, b_other):
    for stride, x, got, keep, send in (
        (4, a, got_a, a_mine, a_other),
        (2, b, got_b, b_mine, b_other),
    ):
        bit = bit_of(stride)
        rows = keep.shape[0]
        for ref, h in ((send, 1 - bit), (keep, bit)):
            ref[...] = x[rows_at(h, rows)] + got[rows_at(h, rows)]


def pair_body(a, got_a, b, got_b, out):
    rows = a.shape[0]
    out[:rows] = a[...] + got_a[...]
    out[rows:] = b[...] + got_b[...]


def unpair_body(x, got, a, b):
    rows = a.shape[0]
    a[...] = x[:rows] + got[:rows]
    b[...] = x[rows:] + got[rows:]


def join_body(a, got_a, b, got_b, a_out, b_out):
    for stride, x, got, out in ((4, a, got_a, a_out), (2, b, got_b, b_out)):
        bit = bit_of(stride)
        rows = x.shape[0]
        out[rows_at(bit, rows)] = x[...]
        out[rows_at(1 - bit, rows)] = got[...]


def join_pair_body(a, got_a, b, got_b, out):
    base = 0
    for stride, x, got in ((2, a, got_a), (4, b, got_b)):
        bit = bit_of(stride)
        rows = x.shape[0]
        for ref, h in ((x, bit), (got, 1 - bit)):
            out[pl.ds(pl.multiple_of(base + h * rows, 16), rows)] = ref[...]
        base += 2 * rows


def swap(x, stride):
    n = lax.axis_size("tiles")
    return lax.ppermute(x, "tiles", [(t, t ^ stride) for t in range(n)])


def bf(rows, like):
    return Shape((rows, like.shape[1]), BF)


class Sum:
    def __init__(self, mine, other, share):
        self.mine, self.got = mine, swap(other, 1)
        self.rows = mine.shape[0]
        self.a = int(share * self.rows / 64) * 64
        self.b = self.rows - self.a

    def step(self, body, rows, args, after, carry):
        outs = [bf(r, self.mine) for r in rows]
        made = call(body, outs, args, after, carry)
        return made[: len(rows)], made[len(rows) :]

    def split(self, after, carry=()):
        rows = [self.a // 2] * 2 + [self.b // 2] * 2
        (a, send_a, b, send_b), carry = self.step(
            split_body, rows, (self.mine, self.got), after, carry
        )
        self.parts = a, swap(send_a, 2), b, swap(send_b, 4)
        return a, *carry

    def halve(self, after, carry=()):
        rows = [self.a // 4] * 2 + [self.b // 4] * 2
        (a, send_a, b, send_b), carry = self.step(halve_body, rows, self.parts, after, carry)
        self.parts = a, swap(send_a, 4), b, swap(send_b, 2)
        return a, *carry

    def pair(self, after, carry=()):
        (m,), carry = self.step(pair_body, [self.rows // 4], self.parts, after, carry)
        token, stride = m, 8
        while 2 * stride < lax.axis_size("tiles"):
            m = m + swap(m, stride)
            stride *= 2
        self.parts = m, swap(m, stride)
        return token, *carry

    def unpair(self, after, carry=()):
        rows = [self.a // 4, self.b // 4]
        (a, b), carry = self.step(unpair_body, rows, self.parts, after, carry)
        self.parts = a, swap(a, 4), b, swap(b, 2)
        return a, *carry

    def join(self, after, carry=()):
        rows = [self.a // 2, self.b // 2]
        (a, b), carry = self.step(join_body, rows, self.parts, after, carry)
        self.parts = a, swap(a, 2), b, swap(b, 4)
        return a, *carry

    def whole(self, after, carry=()):
        (x,), carry = self.step(join_pair_body, [self.rows], self.parts, after, carry)
        return x, *carry


def place_body(slab, flip, *refs):
    x, out, token, wide, sems = refs[0], refs[-4], refs[-3], refs[-2], refs[-1]
    rows = wide.shape[0] // 2
    bit = bit_of(1)
    half = (bit + flip) % 2
    copies = []
    for i in range(2):
        at = slice(i * rows, (i + 1) * rows)
        wide[at] = x[at].astype(F32)
        to = pl.ds(pl.multiple_of(half * 2 * rows + i * rows, rows), rows)
        copies.append(pltpu.make_async_copy(wide.at[at], out.at[slab, to], sems.at[i]))
        copies[-1].start()
    token[...] = jnp.zeros(token.shape, F32)
    for copy in copies:
        copy.wait()


def place(slab, flip, x, shape, held, after):
    hid = shape.shape[1]
    return call(
        functools.partial(place_body, slab, flip),
        (shape, Shape((8, 128), F32)),
        (x,) if held is None else (x, held),
        after,
        specs=[VMEM] if held is None else [VMEM, HBM],
        out_specs=(HBM, VMEM),
        scratch=[pltpu.VMEM((hid // 2, hid), F32), pltpu.SemaphoreType.DMA((2,))],
        aliases={} if held is None else {1: 0},
    )


def finish_body(n, x, got, held, out, lead_out, readout_out, own_out, wide, rest, sems):
    hid = out.shape[1]
    half = hid // 2
    levels = lead_out.shape[0] // 2
    bit = bit_of(1)
    copies = []
    rows = rest.shape[0] // 2
    for i in range(2):
        at = slice(i * half // 2, (i + 1) * half // 2)
        wide[at] = got[at].astype(F32)
        to = pl.ds(pl.multiple_of((1 - bit) * half + i * half // 2, half // 2), half // 2)
        copies.append(pltpu.make_async_copy(wide.at[at], out.at[0, to], sems.at[i]))
        copies[-1].start()
    for ref, b in ((x, bit), (got, 1 - bit)):
        rest[rows_at(b, rows)] = ref[half:].astype(F32)
    a = KEPT + n
    zeros = jnp.zeros((levels - KEPT, hid), F32)
    lead_out[:KEPT] = rest[:KEPT]
    lead_out[KEPT:levels] = zeros
    lead_out[levels : levels + KEPT] = rest[a : a + KEPT]
    lead_out[levels + KEPT :] = zeros
    own_out[...] = rest[pl.ds(KEPT + lax.axis_index("tiles"), 1)]
    readout_out[...] = jnp.concatenate([rest[a + KEPT : a + 2 * KEPT], zeros], 0).T
    for copy in copies:
        copy.wait()


def local(
    warmth,
    brine,
    flags,
    tally,
    assigned,
    desired,
    intercepts,
    leading,
    interior,
    readout,
):
    n = lax.axis_size("tiles")
    lon, lat, levels = warmth.shape
    cols = lon * lat
    hid = leading.shape[1]
    scale = 1.0 / math.sqrt(cols * n)

    up = [(i, (i + 1) % n) for i in range(n)]
    down = [(j, i) for i, j in up]
    wide = (lon, lat, levels)
    depth = jnp.where(flags > 0, tally, 0).astype(F32)
    depth = jnp.broadcast_to(depth[:, :, None], wide)
    owner = jnp.broadcast_to(assigned[:, :, None] + KEPT, wide)
    first = jnp.stack([warmth[:1], brine[:1], depth[:1]])
    last = jnp.stack([warmth[-1:], brine[-1:], depth[-1:]])
    before = lax.ppermute(last, "tiles", up)
    after = lax.ppermute(first, "tiles", down)
    intercepts, _ = lax.optimization_barrier((intercepts, (first, last)))
    bias = lax.all_to_all(
        jnp.broadcast_to(intercepts.reshape(1, hid // 128, 128), (n, hid // 128, 128)),
        "tiles",
        split_axis=0,
        concat_axis=0,
        tiled=True,
    )
    act = Shape((cols, hid), BF)
    half = Shape((hid // 2, hid), BF)
    stepped, feat, wet = call(
        step_body,
        (Shape((2,) + wide, F32), Shape((cols, 2 * levels), BF), Shape((cols, levels), F32)),
        (depth, before, after, owner, warmth, brine),
    )
    weights = pltpu.VMEM((hid, hid), BF)
    sem = pltpu.SemaphoreType.DMA((interior.shape[0],))
    whole_act = pltpu.VMEM(act.shape, BF)
    inferred, act0, act1, slope0, slope1, delta2, other, rest = call(
        functools.partial(forward_body, n, scale),
        (Shape(wide, BF), act, act, act, act, act, half, Shape((KEPT, hid), BF)),
        (feat, wet, bias, desired, leading, interior, readout),
        specs=[VMEM] * 5 + [ANY, VMEM],
        scratch=[
            pltpu.VMEM(leading.shape, BF),
            pltpu.VMEM(interior.shape, BF),
            whole_act,
            whole_act,
            sem,
        ],
        room=ROOM,
    )
    rows = rest_rows(n)
    mine, delta1, below = call(
        middle_body,
        (half, act, half),
        (interior, act0, act1, slope1, delta2),
        specs=[ANY] + [VMEM] * 4,
        scratch=[weights, sem],
        room=ROOM,
    )
    top = Sum(mine, other, TOP_SHARE)
    (token,) = top.split(delta1)
    part = Shape((hid // 2 + rows // 2, hid), BF)
    mine, other = call(
        functools.partial(first_body, n),
        (part, part),
        (interior, feat, act0, slope0, delta1, rest, below),
        token,
        specs=[ANY] + [VMEM] * 6,
        scratch=[whole_act, pltpu.VMEM((rows, hid), BF), weights, sem],
        room=ROOM,
    )
    token, other = top.halve(mine, [other])
    low = Sum(mine, other, LOW_SHARE)
    (token,) = top.pair(token)
    (token,) = low.split(token)
    (token,) = low.halve(token)
    (token,) = top.unpair(token)
    (token,) = low.pair(token)
    (token,) = top.join(token)
    (x,) = top.whole(token)
    token, x = low.unpair(None, [x])
    got = swap(x, 1)
    (token,) = low.join(token)
    grads = Shape((interior.shape[0], hid, hid), F32)
    held, token = place(1, 0, x, grads, None, token)
    held, token = place(1, 1, got, grads, held, token)
    (x,) = low.whole(token)
    held, _ = place(0, 0, x, grads, held, None)
    interior_out, lead_out, readout_out, own_out = call(
        functools.partial(finish_body, n),
        (
            grads,
            Shape((2 * levels, hid), F32),
            Shape((hid, levels), F32),
            Shape((1, hid), F32),
        ),
        (x, swap(x, 1), held),
        specs=[VMEM, VMEM, HBM],
        out_specs=(HBM, VMEM, VMEM, VMEM),
        scratch=[
            pltpu.VMEM((hid // 2, hid), F32),
            pltpu.VMEM((rows, hid), F32),
            pltpu.SemaphoreType.DMA((2,)),
        ],
        aliases={2: 0},
    )
    return stepped, inferred, lead_out, interior_out, readout_out, own_out


def solution(mesh):
    part = ("groups", "tiles")
    return jax.shard_map(
        local,
        mesh=mesh,
        in_specs=(
            P(part, None, None),
            P(part, None, None),
            P(part, None),
            P(part, None),
            P(part, None),
            P(part, None, None),
            P(part, None),
            P(),
            P(),
            P(),
        ),
        out_specs=(
            P(None, part, None, None),
            P(part, None, None),
            P("groups", None),
            P(None, "groups", None),
            P("groups", None),
            P(part, None),
        ),
        check_vma=False,
    )
```

```python
import functools
import math

import jax
import jax.numpy as jnp
from jax import lax
from jax.experimental import pallas as pl
from jax.experimental.pallas import tpu as pltpu
from jax.sharding import PartitionSpec as P

KAPPA = 0.2
KEPT = 80
PACKED = 48
BLOCK = 256
ROOM = 28
BF = jnp.bfloat16
F32 = jnp.float32
VMEM = pl.BlockSpec(memory_space=pltpu.VMEM)
ANY = pl.BlockSpec(memory_space=pl.ANY)
HBM = pl.BlockSpec(memory_space=pltpu.HBM)
Shape = jax.ShapeDtypeStruct


def contract_rows(left, right):
    return lax.dot_general(left, right, (((0,), (0,)), ((), ())), preferred_element_type=F32)


def times_transposed(left, right):
    return lax.dot_general(left, right, (((1,), (1,)), ((), ())), preferred_element_type=F32)


def bit_of(stride):
    return (lax.axis_index("tiles") // stride) % 2


def rows_at(index, rows):
    return pl.ds(pl.multiple_of(index * rows, rows), rows)


def rest_rows(n):
    return -(-(n + 3 * KEPT) // 256) * 256


def call(
    body, outs, args, after=None, carry=(), specs=None, out_specs=None, scratch=(), aliases=None, room=12
):
    outs, args = tuple(outs), tuple(args)
    specs = list(specs or [VMEM] * len(args))
    out_specs = list(out_specs or [VMEM] * len(outs))
    count, made = len(args), len(outs)
    aliases = dict(aliases or {})
    extra = (() if after is None else (after,)) + tuple(carry)
    for i, array in enumerate(carry):
        aliases[count + len(extra) - len(carry) + i] = made + i
    plain = body

    def body(*refs):
        given = refs[:count]
        rest = refs[count + len(extra) :]
        plain(*given, *rest[:made], *rest[made + len(carry) :])

    return pl.pallas_call(
        body,
        out_shape=outs + tuple(Shape(a.shape, a.dtype) for a in carry),
        in_specs=specs + [ANY] * len(extra),
        out_specs=tuple(out_specs + [ANY] * len(carry)),
        scratch_shapes=scratch,
        input_output_aliases=aliases,
        compiler_params=pltpu.CompilerParams(vmem_limit_bytes=room * 2**20),
        cost_estimate=pl.CostEstimate(flops=1, bytes_accessed=1, transcendentals=0),
    )(*args, *extra)


def activate(v):
    s = 0.5 + 0.5 * jnp.tanh(0.5 * v)
    act = v * s
    return act.astype(BF), (s + act * (1.0 - s)).astype(BF)


def step_body(
    depth, near, far, owner, warm_in, brine_in, desired_in, stepped, pack, warm, brine, desired, sems
):
    lon, lat, levels = warm.shape
    cols = lon * lat
    copies = [
        pltpu.make_async_copy(source, ref, sems.at[i])
        for i, (source, ref) in enumerate(
            ((warm_in, warm), (brine_in, brine), (desired_in, desired))
        )
    ]
    for copy in copies:
        copy.start()
    odd = bit_of(1) == 1
    before = jnp.where(odd, near[...], far[...])
    after = jnp.where(odd, far[...], near[...])
    level = lax.broadcasted_iota(jnp.int32, (lon, lat, levels), 2).astype(F32)
    row = lax.broadcasted_iota(jnp.int32, (lon, lat, levels), 1)
    wet = (level < depth[...]).astype(F32)
    wet_b = (level[:1] < before[2]).astype(F32)
    wet_a = (level[:1] < after[2]).astype(F32)
    wet_e = jnp.concatenate([wet[1:], wet_a], 0)
    wet_w = jnp.concatenate([wet_b, wet[:-1]], 0)
    wet_n = jnp.where(row < lat - 1, pltpu.roll(wet, lat - 1, 1), 0.0)
    wet_s = jnp.where(row > 0, pltpu.roll(wet, 1, 1), 0.0)
    lane = lax.broadcasted_iota(jnp.int32, (cols, levels), 1)
    for copy in copies:
        copy.wait()
    target = desired[...].reshape(cols, levels).astype(F32)
    for i, ref in enumerate((warm, brine)):
        q = ref[...]
        total = wet_e * (jnp.concatenate([q[1:], after[i]], 0) - q)
        total = total + wet_w * (jnp.concatenate([before[i], q[:-1]], 0) - q)
        total = total + wet_n * (pltpu.roll(q, lat - 1, 1) - q)
        total = total + wet_s * (pltpu.roll(q, 1, 1) - q)
        out = q + KAPPA * wet * total
        stepped[i] = out
        group = (out * wet).reshape(cols, levels)
        if i == 0:
            group = jnp.where(lane == KEPT - 2, owner[...].reshape(cols, levels), group)
            group = jnp.where(lane == KEPT - 1, depth[...].reshape(cols, levels), group)
        beside = pltpu.roll(target, (KEPT - i * PACKED) % levels, 1)
        group = jnp.where(lane >= KEPT, beside, group)
        pack[:, i * levels : (i + 1) * levels] = group.astype(BF)


def weight_grad(pairs, at):
    total = None
    for act, delta in pairs:
        term = contract_rows(act[:, at], delta[...])
        total = term if total is None else total + term
    return total.astype(BF)


def back_through(delta, weights, slope, out):
    for j in range(0, out.shape[1], BLOCK):
        back = times_transposed(delta, weights[j : j + BLOCK])
        out[:, j : j + BLOCK] = (back * slope[:, j : j + BLOCK].astype(F32)).astype(BF)


def train(scale, pack, interior, readout, inferred, outs, scratch, weights):
    act0, act1, slope0, slope1, delta2, feat, rest = outs
    w_int, w_out, act2, slope2, sems = scratch
    cols = pack.shape[0]
    levels = pack.shape[1] // 2
    hid = readout.shape[0]
    deep = interior.shape[0]
    start_weights, w_lead = weights
    start_weights()
    copies = [
        pltpu.make_async_copy(interior.at[i], w_int.at[i], sems.at[i]) for i in range(deep)
    ]
    copies.append(pltpu.make_async_copy(readout, w_out, sems.at[deep]))
    for copy in copies:
        copy.start()
    groups = [pack[:, i * levels : (i + 1) * levels].astype(F32) for i in range(2)]
    lane = lax.broadcasted_iota(jnp.int32, (cols, levels), 1)
    own = lane.astype(F32) == groups[0][:, KEPT - 2 : KEPT - 1] + KEPT
    wet = lane.astype(F32) < groups[0][:, KEPT - 1 : KEPT]
    target = jnp.where(
        lane < PACKED,
        pltpu.roll(groups[0], levels - KEPT, 1),
        pltpu.roll(groups[1], levels - KEPT + PACKED, 1),
    )
    for i, group in enumerate(groups):
        hot = jnp.where(own, 1.0, 0.0)
        feat[:, i * levels : (i + 1) * levels] = jnp.where(lane < KEPT - 2, group, hot).astype(BF)
    w_lead = w_lead()
    for layer, (left, right, act, slope) in enumerate(
        (
            (feat, w_lead, act0, slope0),
            (act0, w_int.at[0], act1, slope1),
            (act1, w_int.at[1], act2, slope2),
        )
    ):
        if layer:
            copies[layer - 1].wait()
        for j in range(0, hid, BLOCK):
            pre = jnp.dot(left[...], right[:, j : j + BLOCK], preferred_element_type=F32)
            act[:, j : j + BLOCK], slope[:, j : j + BLOCK] = activate(pre)
    copies[deep].wait()
    output = jnp.dot(act2[...], w_out[...], preferred_element_type=F32)
    if inferred is not None:
        inferred[...] = output.astype(BF).reshape(inferred.shape)
    err = jnp.where(wet, (output - target) * scale, 0.0).astype(BF)
    back_through(err, w_out, slope2, delta2)
    rest[...] = contract_rows(err, act2[...])[:KEPT]


def forward_body(n, scale, pack, bias, leading, interior, readout, *refs):
    inferred, w_lead, refs = refs[0], refs[1], refs[2:]
    copy = pltpu.make_async_copy(leading, w_lead, refs[-1].at[interior.shape[0] + 1])

    def weights():
        copy.wait()
        for j in range(bias.shape[1]):
            value = bias[:, j]
            high = value.astype(BF)
            at = slice(j * bias.shape[2], (j + 1) * bias.shape[2])
            low = (value - high.astype(F32)).astype(BF)
            w_lead[KEPT : KEPT + n, at] = high
            w_lead[bias.shape[2] + KEPT : bias.shape[2] + KEPT + n, at] = low
        return w_lead

    train(scale, pack, interior, readout, inferred, refs[:7], refs[7:], (copy.start, weights))


def partner_body(
    scale, pack, w_lead, interior, readout, act1, delta2, *refs
):
    outs, other, scratch = refs[:7], refs[7], refs[8:]
    train(
        scale, pack, interior, readout, None, outs, scratch, (lambda: None, lambda: w_lead)
    )
    rows = other.shape[0]
    at = pl.ds(pl.multiple_of((1 - bit_of(1)) * 2 * rows + bit_of(4) * rows, rows), rows)
    other[...] = weight_grad(((act1, delta2), (outs[1], outs[4])), at)


def middle_body(
    interior, act1, delta2, act1_p, delta2_p, slope1, mine, delta1, w_int, sems
):
    copy = pltpu.make_async_copy(interior.at[1], w_int, sems.at[0])
    copy.start()
    rows = mine.shape[0]
    at = pl.ds(pl.multiple_of(bit_of(1) * 2 * rows + bit_of(4) * rows, rows), rows)
    mine[...] = weight_grad(((act1, delta2), (act1_p, delta2_p)), at)
    copy.wait()
    back_through(delta2[...], w_int, slope1, delta1)


def first_body(
    n,
    interior,
    feat,
    act0,
    slope0,
    delta1,
    rest_in,
    feat_p,
    act0_p,
    slope0_p,
    slope1_p,
    delta2_p,
    rest_p,
    mine,
    other_0,
    other_1,
    other_2,
    other_3,
    delta1_p,
    delta0,
    delta0_p,
    rest,
    spare,
    w_int,
    sems,
):
    levels = feat.shape[1] // 2
    hid = slope0.shape[1]
    copies = [
        pltpu.make_async_copy(interior.at[i], w_int.at[i], sems.at[i])
        for i in range(interior.shape[0])
    ]
    for copy in reversed(copies):
        copy.start()
    copies[1].wait()
    back_through(delta2_p[...], w_int.at[1], slope1_p, delta1_p)
    copies[0].wait()
    back_through(delta1[...], w_int.at[0], slope0, delta0)
    back_through(delta1_p[...], w_int.at[0], slope0_p, delta0_p)
    total = contract_rows(feat[...], delta0[...]) + contract_rows(feat_p[...], delta0_p[...])
    lead = total.astype(BF)
    a = KEPT + n
    rest[:a] = lead[:a]
    rest[a : a + KEPT] = lead[levels : levels + KEPT]
    rest[a + KEPT : a + 2 * KEPT] = (rest_in[...] + rest_p[...]).astype(BF)
    rows = rest.shape[0]
    if rows > a + 2 * KEPT:
        rest[a + 2 * KEPT :] = jnp.zeros((rows - a - 2 * KEPT, hid), BF)
    bit, z = bit_of(1), bit_of(4)
    quarter, part = hid // 8, rows // 8
    for ref, b in ((spare, 1 - bit), (mine, bit)):
        at = pl.ds(pl.multiple_of((b * 2 + z) * 2 * quarter, 2 * quarter), 2 * quarter)
        got = weight_grad(((act0, delta1), (act0_p, delta1_p)), at)
        for y in range(2):
            base = y * (quarter + part)
            ref[base : base + quarter] = got[y * quarter : (y + 1) * quarter]
            from_rest = pl.ds(pl.multiple_of((b * 2 + z) * 2 * part + y * part, part), part)
            ref[base + quarter : base + quarter + part] = rest[from_rest]
    for i, ref in enumerate((other_0, other_1, other_2, other_3)):
        ref[...] = spare[i * ref.shape[0] : (i + 1) * ref.shape[0]]


def split_body(count, mine, *refs):
    got, keep, sends, total = refs[:count], refs[count], refs[count + 1 : -1], refs[-1]
    base = 0
    for ref in got:
        at = slice(base, base + ref.shape[0])
        total[at] = mine[at] + ref[...]
        base += ref.shape[0]
    bit = bit_of(2)
    rows = keep.shape[0]
    keep[...] = total[rows_at(bit, rows)]
    for i, send in enumerate(sends):
        part = send.shape[0]
        at = pl.ds(pl.multiple_of((1 - bit) * rows + i * part, 16), part)
        send[...] = total[at]


def pair_body(keep, *refs):
    got, out = refs[:-1], refs[-1]
    base = 0
    for ref in got:
        at = slice(base, base + ref.shape[0])
        out[at] = keep[at] + ref[...]
        base += ref.shape[0]


def unpair_body(x, got, a, b):
    rows = a.shape[0]
    a[...] = x[:rows] + got[:rows]
    b[...] = x[rows:] + got[rows:]


def join_body(a, got_a, b, got_b, a_out, b_out):
    for stride, x, got, out in ((4, a, got_a, a_out), (2, b, got_b, b_out)):
        bit = bit_of(stride)
        rows = x.shape[0]
        out[rows_at(bit, rows)] = x[...]
        out[rows_at(1 - bit, rows)] = got[...]


def whole_body(a, got_a, b, got_b, out):
    rows = a.shape[0] // 2
    y, z = bit_of(2), bit_of(4)

    def at(z, y, low):
        return pl.ds(pl.multiple_of((z * 2 + y) * 2 * rows + low * rows, 16), rows)

    for i in range(2):
        own = slice(i * rows, (i + 1) * rows)
        out[at(i, y, 0)] = a[own]
        out[at(i, 1 - y, 0)] = got_a[own]
        out[at(z, i, 1)] = b[own]
        out[at(1 - z, i, 1)] = got_b[own]


def swap(x, stride):
    n = lax.axis_size("tiles")
    return lax.ppermute(x, "tiles", [(t, t ^ stride) for t in range(n)])


def bf(rows, like):
    return Shape((rows, like.shape[1]), BF)


class Sum:
    def __init__(self, mine, others, sends):
        self.mine, self.got = mine, [swap(other, 1) for other in others]
        self.rows, self.sends = mine.shape[0], sends

    def step(self, body, rows, args, after, carry=(), scratch=()):
        outs = [bf(r, self.mine) for r in rows]
        made = call(body, outs, args, after, carry, scratch=scratch)
        return made[: len(rows)], made[len(rows) :]

    def split(self, after, carry=()):
        half = self.rows // 2
        (keep, *sends), carry = self.step(
            functools.partial(split_body, len(self.got)),
            [half] + [half // self.sends] * self.sends,
            (self.mine, *self.got),
            after,
            carry,
            [pltpu.VMEM(self.mine.shape, BF)],
        )
        self.parts = (keep, *[swap(send, 2) for send in sends])
        return keep, *carry

    def pair(self, after, carry=()):
        (m,), carry = self.step(pair_body, [self.rows // 2], self.parts, after, carry)
        token, stride = m, 8
        while 2 * stride < lax.axis_size("tiles"):
            m = m + swap(m, stride)
            stride *= 2
        self.parts = m, swap(m, stride)
        return token, *carry

    def unpair(self, after, carry=()):
        (a, b), carry = self.step(unpair_body, [self.rows // 4] * 2, self.parts, after, carry)
        self.parts = a, swap(a, 4), b, swap(b, 2)
        return a, *carry

    def join(self, after, carry=()):
        (a, b), carry = self.step(join_body, [self.rows // 2] * 2, self.parts, after, carry)
        self.parts = a, swap(a, 2), b, swap(b, 4)
        return a, *carry

    def whole(self, after, carry=()):
        (x,), carry = self.step(whole_body, [2 * self.rows], self.parts, after, carry)
        return x, *carry


def place_rows(x, half, slab, out, wide, sems):
    count = x.shape[0] // 4
    rows = wide.shape[0] // 4
    copies = []
    for i in range(4):
        at = slice(i * rows, (i + 1) * rows)
        wide[at] = x[i * count : i * count + rows].astype(F32)
        to = pl.ds(pl.multiple_of(half * 4 * rows + i * rows, rows), rows)
        copies.append(pltpu.make_async_copy(wide.at[at], out.at[slab, to], sems.at[i]))
        copies[-1].start()
    return copies


def place_body(slab, flip, *refs):
    x, out, token, wide, sems = refs[0], refs[-4], refs[-3], refs[-2], refs[-1]
    copies = place_rows(x, (bit_of(1) + flip) % 2, slab, out, wide, sems)
    token[...] = jnp.zeros(token.shape, F32)
    for copy in copies:
        copy.wait()


def place(slab, flip, x, shape, held, after):
    hid = shape.shape[1]
    return call(
        functools.partial(place_body, slab, flip),
        (shape, Shape((8, 128), F32)),
        (x,) if held is None else (x, held),
        after,
        specs=[VMEM] if held is None else [VMEM, HBM],
        out_specs=(HBM, VMEM),
        scratch=[pltpu.VMEM((hid // 2, hid), F32), pltpu.SemaphoreType.DMA((4,))],
        aliases={} if held is None else {1: 0},
    )


def finish_body(n, x, got, held, out, lead_out, readout_out, own_out, wide, rest, sems):
    hid = out.shape[1]
    levels = lead_out.shape[0] // 2
    bit = bit_of(1)
    copies = place_rows(got, 1 - bit, 0, out, wide, sems)
    quarter, part = hid // 8, rest.shape[0] // 8
    for ref, b in ((x, bit), (got, 1 - bit)):
        for i in range(4):
            at = pl.ds(pl.multiple_of(b * 4 * part + i * part, part), part)
            base = i * (quarter + part) + quarter
            rest[at] = ref[base : base + part].astype(F32)
    a = KEPT + n
    zeros = jnp.zeros((levels - KEPT, hid), F32)
    lead_out[: KEPT - 2] = rest[: KEPT - 2]
    lead_out[KEPT - 2 : levels] = jnp.zeros((levels - KEPT + 2, hid), F32)
    lead_out[levels : levels + KEPT] = rest[a : a + KEPT]
    lead_out[levels + KEPT :] = zeros
    own_out[...] = rest[pl.ds(KEPT + lax.axis_index("tiles"), 1)]
    readout_out[...] = jnp.concatenate([rest[a + KEPT : a + 2 * KEPT], zeros], 0).T
    for copy in copies:
        copy.wait()


def local(
    warmth,
    brine,
    flags,
    tally,
    assigned,
    desired,
    intercepts,
    leading,
    interior,
    readout,
):
    n = lax.axis_size("tiles")
    lon, lat, levels = warmth.shape
    cols = lon * lat
    hid = leading.shape[1]
    scale = 1.0 / math.sqrt(cols * n)

    wide = (lon, lat, levels)
    depth = jnp.where(flags > 0, tally, 0).astype(F32)
    depth = jnp.broadcast_to(depth[:, :, None], wide)
    owner = jnp.broadcast_to(assigned[:, :, None].astype(F32), wide)
    odd = bit_of(1) == 1
    first = jnp.stack([warmth[:1], brine[:1], depth[:1]])
    last = jnp.stack([warmth[-1:], brine[-1:], depth[-1:]])
    near = swap(jnp.where(odd, first, last), 1)
    pairs = [(t, (t + 1) % n if t % 2 else (t - 1) % n) for t in range(n)]
    far = lax.ppermute(jnp.where(odd, last, first), "tiles", pairs)
    bias = lax.all_to_all(
        jnp.broadcast_to(intercepts.reshape(1, hid // 128, 128), (n, hid // 128, 128)),
        "tiles",
        split_axis=0,
        concat_axis=0,
        tiled=True,
    )
    warmth, brine, desired, leading, interior, readout = [
        pltpu.with_memory_space_constraint(a, pltpu.HBM)
        for a in (warmth, brine, desired, leading, interior, readout)
    ]
    stepped, pack = call(
        step_body,
        (Shape((2,) + wide, F32), Shape((cols, 2 * levels), BF)),
        (depth, near, far, owner, warmth, brine, desired),
        bias,
        specs=[VMEM] * 4 + [HBM] * 3,
        scratch=[
            pltpu.VMEM(wide, F32),
            pltpu.VMEM(wide, F32),
            pltpu.VMEM(wide, BF),
            pltpu.SemaphoreType.DMA((3,)),
        ],
    )
    pack_p = swap(pack, 4)
    act = Shape((cols, hid), BF)
    one = pltpu.VMEM(act.shape, BF)
    sem = pltpu.SemaphoreType.DMA((interior.shape[0] + 2,))
    trained = (act,) * 5 + (Shape(pack.shape, BF), Shape((KEPT, hid), F32))
    scratch = [pltpu.VMEM(interior.shape, BF), pltpu.VMEM(readout.shape, BF), one, one, sem]
    inferred, w_lead, act0, act1, slope0, slope1, delta2, feat, rest = call(
        functools.partial(forward_body, n, scale),
        (Shape(wide, BF), Shape(leading.shape, BF)) + trained,
        (pack, bias, leading, interior, readout),
        specs=[VMEM] * 2 + [HBM] * 3,
        scratch=scratch,
        room=ROOM,
    )
    half = Shape((hid // 4, hid), BF)
    act0_p, act1_p, slope0_p, slope1_p, delta2_p, feat_p, rest_p, other = call(
        functools.partial(partner_body, scale),
        trained + (half,),
        (pack_p, w_lead, interior, readout, act1, delta2),
        specs=[VMEM] * 2 + [HBM] * 2 + [VMEM] * 2,
        scratch=scratch,
        room=ROOM,
    )
    mine, delta1 = call(
        middle_body,
        (half, act),
        (interior, act1, delta2, act1_p, delta2_p, slope1),
        specs=[HBM] + [VMEM] * 5,
        scratch=[pltpu.VMEM((hid, hid), BF), sem],
        room=ROOM,
    )
    top = Sum(mine, [other], 1)
    (token,) = top.split(delta1)
    rows = rest_rows(n)
    part = Shape((hid // 4 + rows // 4, hid), BF)
    mine, *others = call(
        functools.partial(first_body, n),
        (part,) + (bf(part.shape[0] // 4, part),) * 4,
        (
            interior,
            feat,
            act0,
            slope0,
            delta1,
            rest,
            feat_p,
            act0_p,
            slope0_p,
            slope1_p,
            delta2_p,
            rest_p,
        ),
        token,
        specs=[HBM] + [VMEM] * 11,
        scratch=[
            *[one] * 3,
            pltpu.VMEM((rows, hid), BF),
            pltpu.VMEM(part.shape, BF),
            pltpu.VMEM(interior.shape, BF),
            sem,
        ],
        room=ROOM,
    )
    low = Sum(mine, others, 2)
    (token,) = top.pair(mine)
    (token,) = low.split(token)
    (token,) = top.unpair(token)
    (token,) = low.pair(token)
    (token,) = top.join(token)
    (token,) = low.unpair(token)
    (x,) = top.whole(token)
    grads = Shape((interior.shape[0], hid, hid), F32)
    token, x = low.join(None, [x])
    held, token = place(1, 0, x, grads, None, token)
    held, token = place(1, 1, swap(x, 1), grads, held, token)
    (y,) = low.whole(token)
    held, _ = place(0, 0, y, grads, held, None)
    interior_out, lead_out, readout_out, own_out = call(
        functools.partial(finish_body, n),
        (
            grads,
            Shape((2 * levels, hid), F32),
            Shape((hid, levels), F32),
            Shape((1, hid), F32),
        ),
        (y, swap(y, 1), held),
        specs=[VMEM, VMEM, HBM],
        out_specs=(HBM, VMEM, VMEM, VMEM),
        scratch=[
            pltpu.VMEM((hid // 2, hid), F32),
            pltpu.VMEM((rows, hid), F32),
            pltpu.SemaphoreType.DMA((4,)),
        ],
        aliases={2: 0},
    )
    return stepped, inferred, lead_out, interior_out, readout_out, own_out


def solution(mesh):
    part = ("groups", "tiles")
    return jax.shard_map(
        local,
        mesh=mesh,
        in_specs=(
            P(part, None, None),
            P(part, None, None),
            P(part, None),
            P(part, None),
            P(part, None),
            P(part, None, None),
            P(part, None),
            P(),
            P(),
            P(),
        ),
        out_specs=(
            P(None, part, None, None),
            P(part, None, None),
            P("groups", None),
            P(None, "groups", None),
            P("groups", None),
            P(part, None),
        ),
        check_vma=False,
    )
```

```python
import functools
import math

import jax
import jax.numpy as jnp
from jax import lax
from jax.experimental import pallas as pl
from jax.experimental.pallas import tpu as pltpu
from jax.sharding import PartitionSpec as P

KAPPA = 0.2
KEPT = 80
PACKED = 48
BLOCK = 256
ROOM = 28
TOP_SHARE = 0.625
LOW_SHARE = 0.5
LOW_MIDS = 2
BF = jnp.bfloat16
F32 = jnp.float32
VMEM = pl.BlockSpec(memory_space=pltpu.VMEM)
ANY = pl.BlockSpec(memory_space=pl.ANY)
HBM = pl.BlockSpec(memory_space=pltpu.HBM)
Shape = jax.ShapeDtypeStruct


def contract_rows(left, right):
    return lax.dot_general(left, right, (((0,), (0,)), ((), ())), preferred_element_type=F32)


def times_transposed(left, right):
    return lax.dot_general(left, right, (((1,), (1,)), ((), ())), preferred_element_type=F32)


def bit_of(stride):
    return (lax.axis_index("tiles") // stride) % 2


def rows_at(index, rows):
    return pl.ds(pl.multiple_of(index * rows, rows), rows)


def rest_rows(n):
    return -(-(n + 3 * KEPT) // 256) * 256


def call(
    body, outs, args, after=None, carry=(), specs=None, out_specs=None, scratch=(), aliases=None, room=12
):
    outs, args = tuple(outs), tuple(args)
    specs = list(specs or [VMEM] * len(args))
    out_specs = list(out_specs or [VMEM] * len(outs))
    count, made = len(args), len(outs)
    aliases = dict(aliases or {})
    extra = (() if after is None else (after,)) + tuple(carry)
    for i, array in enumerate(carry):
        aliases[count + len(extra) - len(carry) + i] = made + i
    plain = body

    def body(*refs):
        given = refs[:count]
        rest = refs[count + len(extra) :]
        plain(*given, *rest[:made], *rest[made + len(carry) :])

    return pl.pallas_call(
        body,
        out_shape=outs + tuple(Shape(a.shape, a.dtype) for a in carry),
        in_specs=specs + [ANY] * len(extra),
        out_specs=tuple(out_specs + [ANY] * len(carry)),
        scratch_shapes=scratch,
        input_output_aliases=aliases,
        compiler_params=pltpu.CompilerParams(vmem_limit_bytes=room * 2**20),
        cost_estimate=pl.CostEstimate(flops=1, bytes_accessed=1, transcendentals=0),
    )(*args, *extra)


def activate(v):
    v = v.astype(BF)
    s = 0.5 + 0.5 * jnp.tanh(0.5 * v)
    act = v * s
    return act, s + act * (1.0 - s)


def stage_body(*refs):
    count = len(refs) // 2
    copies = [
        pltpu.make_async_copy(refs[i], refs[count + i], refs[-1].at[i]) for i in range(count)
    ]
    for copy in copies:
        copy.start()
    for copy in copies:
        copy.wait()


def step_body(depth, near, far, owner, warm, brine, desired, stepped, pack):
    lon, lat, levels = warm.shape
    cols = lon * lat
    odd = bit_of(1) == 1
    before = jnp.where(odd, near[...], far[...])
    after = jnp.where(odd, far[...], near[...])
    level = lax.broadcasted_iota(jnp.int32, (lon, lat, levels), 2).astype(F32)
    row = lax.broadcasted_iota(jnp.int32, (lon, lat, levels), 1)
    wet = (level < depth[...]).astype(F32)
    wet_b = (level[:1] < before[2]).astype(F32)
    wet_a = (level[:1] < after[2]).astype(F32)
    wet_e = jnp.concatenate([wet[1:], wet_a], 0)
    wet_w = jnp.concatenate([wet_b, wet[:-1]], 0)
    wet_n = jnp.where(row < lat - 1, pltpu.roll(wet, lat - 1, 1), 0.0)
    wet_s = jnp.where(row > 0, pltpu.roll(wet, 1, 1), 0.0)
    lane = lax.broadcasted_iota(jnp.int32, (cols, levels), 1)
    target = desired[...].reshape(cols, levels).astype(F32)
    for i, ref in enumerate((warm, brine)):
        q = ref[...]
        total = wet_e * (jnp.concatenate([q[1:], after[i]], 0) - q)
        total = total + wet_w * (jnp.concatenate([before[i], q[:-1]], 0) - q)
        total = total + wet_n * (pltpu.roll(q, lat - 1, 1) - q)
        total = total + wet_s * (pltpu.roll(q, 1, 1) - q)
        out = q + KAPPA * wet * total
        stepped[i] = out
        group = (out * wet).reshape(cols, levels)
        if i == 0:
            group = jnp.where(lane == KEPT - 2, owner[...].reshape(cols, levels), group)
            group = jnp.where(lane == KEPT - 1, depth[...].reshape(cols, levels), group)
        beside = pltpu.roll(target, (KEPT - i * PACKED) % levels, 1)
        group = jnp.where(lane >= KEPT, beside, group)
        pack[:, i * levels : (i + 1) * levels] = group.astype(BF)


def weight_grad(pairs, at):
    total = None
    for act, delta in pairs:
        term = contract_rows(act[:, at], delta[...])
        total = term if total is None else total + term
    return total.astype(BF)


def back_through(delta, weights, slope, out):
    for j in range(0, out.shape[1], BLOCK):
        back = times_transposed(delta, weights[j : j + BLOCK])
        out[:, j : j + BLOCK] = (back * slope[:, j : j + BLOCK].astype(F32)).astype(BF)


def train(scale, pack, interior, readout, inferred, outs, scratch, weights):
    act0, act1, slope0, slope1, delta2, feat, rest = outs
    w_int, w_out, act2, slope2, sems = scratch
    cols = pack.shape[0]
    levels = pack.shape[1] // 2
    hid = readout.shape[0]
    deep = interior.shape[0]
    start_weights, w_lead = weights
    start_weights()
    copies = [
        pltpu.make_async_copy(interior.at[i], w_int.at[i], sems.at[i]) for i in range(deep)
    ]
    copies.append(pltpu.make_async_copy(readout, w_out, sems.at[deep]))
    for copy in copies:
        copy.start()
    groups = [pack[:, i * levels : (i + 1) * levels].astype(F32) for i in range(2)]
    lane = lax.broadcasted_iota(jnp.int32, (cols, levels), 1)
    own = lane.astype(F32) == groups[0][:, KEPT - 2 : KEPT - 1] + KEPT
    wet = lane.astype(F32) < groups[0][:, KEPT - 1 : KEPT]
    target = jnp.where(
        lane < PACKED,
        pltpu.roll(groups[0], levels - KEPT, 1),
        pltpu.roll(groups[1], levels - KEPT + PACKED, 1),
    )
    for i, group in enumerate(groups):
        hot = jnp.where(own, 1.0, 0.0)
        feat[:, i * levels : (i + 1) * levels] = jnp.where(lane < KEPT - 2, group, hot).astype(BF)
    w_lead = w_lead()
    for layer, (left, right, act, slope) in enumerate(
        (
            (feat, w_lead, act0, slope0),
            (act0, w_int.at[0], act1, slope1),
            (act1, w_int.at[1], act2, slope2),
        )
    ):
        if layer:
            copies[layer - 1].wait()
        for j in range(0, hid, BLOCK):
            pre = jnp.dot(left[...], right[:, j : j + BLOCK], preferred_element_type=F32)
            act[:, j : j + BLOCK], slope[:, j : j + BLOCK] = activate(pre)
    copies[deep].wait()
    output = jnp.dot(act2[...], w_out[...], preferred_element_type=F32)
    if inferred is not None:
        inferred[...] = output.astype(BF).reshape(inferred.shape)
    err = jnp.where(wet, (output - target) * scale, 0.0).astype(BF)
    back_through(err, w_out, slope2, delta2)
    rest[...] = contract_rows(err, act2[...])[:KEPT]


def forward_body(n, scale, pack, bias, leading, interior, readout, *refs):
    inferred, w_lead, refs = refs[0], refs[1], refs[2:]
    copy = pltpu.make_async_copy(leading, w_lead, refs[-1].at[interior.shape[0] + 1])

    def weights():
        copy.wait()
        for j in range(bias.shape[1]):
            value = bias[:, j]
            high = value.astype(BF)
            at = slice(j * bias.shape[2], (j + 1) * bias.shape[2])
            low = (value - high.astype(F32)).astype(BF)
            w_lead[KEPT : KEPT + n, at] = high
            w_lead[bias.shape[2] + KEPT : bias.shape[2] + KEPT + n, at] = low
        return w_lead

    train(scale, pack, interior, readout, inferred, refs[:7], refs[7:], (copy.start, weights))


def partner_body(
    scale, pack, w_lead, interior, readout, act1, delta2, *refs
):
    outs, other, scratch = refs[:7], refs[7], refs[8:]
    train(
        scale, pack, interior, readout, None, outs, scratch, (lambda: None, lambda: w_lead)
    )
    rows = other.shape[0]
    at = pl.ds(pl.multiple_of((1 - bit_of(1)) * 2 * rows + bit_of(4) * rows, rows), rows)
    other[...] = weight_grad(((act1, delta2), (outs[1], outs[4])), at)


def middle_body(
    interior, act1, delta2, act1_p, delta2_p, slope1, mine, delta1, w_int, sems
):
    copy = pltpu.make_async_copy(interior.at[1], w_int, sems.at[0])
    copy.start()
    rows = mine.shape[0]
    at = pl.ds(pl.multiple_of(bit_of(1) * 2 * rows + bit_of(4) * rows, rows), rows)
    mine[...] = weight_grad(((act1, delta2), (act1_p, delta2_p)), at)
    copy.wait()
    back_through(delta2[...], w_int, slope1, delta1)


def first_body(
    n,
    interior,
    feat,
    act0,
    slope0,
    delta1,
    rest_in,
    feat_p,
    act0_p,
    slope0_p,
    slope1_p,
    delta2_p,
    rest_p,
    mine,
    other_0,
    other_1,
    other_2,
    other_3,
    delta1_p,
    delta0,
    delta0_p,
    rest,
    spare,
    w_int,
    sems,
):
    levels = feat.shape[1] // 2
    hid = slope0.shape[1]
    copies = [
        pltpu.make_async_copy(interior.at[i], w_int.at[i], sems.at[i])
        for i in range(interior.shape[0])
    ]
    for copy in reversed(copies):
        copy.start()
    copies[1].wait()
    back_through(delta2_p[...], w_int.at[1], slope1_p, delta1_p)
    copies[0].wait()
    back_through(delta1[...], w_int.at[0], slope0, delta0)
    back_through(delta1_p[...], w_int.at[0], slope0_p, delta0_p)
    total = contract_rows(feat[...], delta0[...]) + contract_rows(feat_p[...], delta0_p[...])
    lead = total.astype(BF)
    a = KEPT + n
    rest[:a] = lead[:a]
    rest[a : a + KEPT] = lead[levels : levels + KEPT]
    rest[a + KEPT : a + 2 * KEPT] = (rest_in[...] + rest_p[...]).astype(BF)
    rows = rest.shape[0]
    if rows > a + 2 * KEPT:
        rest[a + 2 * KEPT :] = jnp.zeros((rows - a - 2 * KEPT, hid), BF)
    bit, z = bit_of(1), bit_of(4)
    quarter, part = hid // 8, rows // 8
    for ref, b in ((spare, 1 - bit), (mine, bit)):
        at = pl.ds(pl.multiple_of((b * 2 + z) * 2 * quarter, 2 * quarter), 2 * quarter)
        got = weight_grad(((act0, delta1), (act0_p, delta1_p)), at)
        for y in range(2):
            base = y * (quarter + part)
            ref[base : base + quarter] = got[y * quarter : (y + 1) * quarter]
            from_rest = pl.ds(pl.multiple_of((b * 2 + z) * 2 * part + y * part, part), part)
            ref[base + quarter : base + quarter + part] = rest[from_rest]
    for i, ref in enumerate((other_0, other_1, other_2, other_3)):
        ref[...] = spare[i * ref.shape[0] : (i + 1) * ref.shape[0]]


def split_body(count, mine, *refs):
    got, keep, sends, total = refs[:count], refs[count], refs[count + 1 : -1], refs[-1]
    base = 0
    for ref in got:
        at = slice(base, base + ref.shape[0])
        total[at] = mine[at] + ref[...]
        base += ref.shape[0]
    bit = bit_of(2)
    rows = keep.shape[0]
    keep[...] = total[rows_at(bit, rows)]
    for i, send in enumerate(sends):
        part = send.shape[0]
        at = pl.ds(pl.multiple_of((1 - bit) * rows + i * part, 16), part)
        send[...] = total[at]


def rows_of(refs):
    base, places = 0, []
    for ref in refs:
        places.append(slice(base, base + ref.shape[0]))
        base += ref.shape[0]
    return places


def pair_body(count, keep, *refs):
    got, outs, total = refs[:count], refs[count:-1], refs[-1]
    for ref, at in zip(got, rows_of(got)):
        total[at] = keep[at] + ref[...]
    for ref, at in zip(outs, rows_of(outs)):
        ref[...] = total[at]


def unpair_body(count, *refs):
    own, got, (a, b, total) = refs[:count], refs[count : 2 * count], refs[2 * count :]
    for x, ref, at in zip(own, got, rows_of(own)):
        total[at] = x[...] + ref[...]
    for ref, at in zip((a, b), rows_of((a, b))):
        ref[...] = total[at]


def join_body(a, got_a, b, got_b, a_out, b_out):
    for stride, x, got, out in ((4, a, got_a, a_out), (2, b, got_b, b_out)):
        bit = bit_of(stride)
        rows = x.shape[0]
        out[rows_at(bit, rows)] = x[...]
        out[rows_at(1 - bit, rows)] = got[...]


def whole_body(a, got_a, b, got_b, out):
    rows = a.shape[0] // 2, b.shape[0] // 2
    y, z = bit_of(2), bit_of(4)

    def at(z, y, low):
        base = (z * 2 + y) * (rows[0] + rows[1]) + low * rows[0]
        return pl.ds(pl.multiple_of(base, 16), rows[low])

    for i in range(2):
        own = slice(i * rows[0], (i + 1) * rows[0])
        out[at(i, y, 0)] = a[own]
        out[at(i, 1 - y, 0)] = got_a[own]
        own = slice(i * rows[1], (i + 1) * rows[1])
        out[at(z, i, 1)] = b[own]
        out[at(1 - z, i, 1)] = got_b[own]


def swap(x, stride):
    n = lax.axis_size("tiles")
    return lax.ppermute(x, "tiles", [(t, t ^ stride) for t in range(n)])


def bf(rows, like):
    return Shape((rows, like.shape[1]), BF)


class Sum:
    def __init__(self, mine, others, sends, mids, share):
        self.mine, self.got = mine, [swap(other, 1) for other in others]
        self.rows, self.sends, self.mids = mine.shape[0], sends, mids
        self.a = int(share * self.rows / 32) * 16
        self.b = self.rows // 2 - self.a

    def step(self, body, rows, args, after, carry=(), scratch=()):
        outs = [bf(r, self.mine) for r in rows]
        made = call(body, outs, args, after, carry, scratch=scratch)
        return made[: len(rows)], made[len(rows) :]

    def split(self, after, carry=()):
        half = self.rows // 2
        (keep, *sends), carry = self.step(
            functools.partial(split_body, len(self.got)),
            [half] + [half // self.sends] * self.sends,
            (self.mine, *self.got),
            after,
            carry,
            [pltpu.VMEM(self.mine.shape, BF)],
        )
        self.parts = (keep, *[swap(send, 2) for send in sends])
        return keep, *carry

    def pair(self, after, carry=()):
        half = self.rows // 2
        m, carry = self.step(
            functools.partial(pair_body, len(self.parts) - 1),
            [half // self.mids] * self.mids,
            self.parts,
            after,
            carry,
            [pltpu.VMEM((half, self.mine.shape[1]), BF)],
        )
        token, stride = m[0], 8
        while 2 * stride < lax.axis_size("tiles"):
            m = [x + swap(x, stride) for x in m]
            stride *= 2
        self.parts = (*m, *[swap(x, stride) for x in m])
        return token, *carry

    def unpair(self, after, carry=()):
        (a, b), carry = self.step(
            functools.partial(unpair_body, self.mids),
            [self.a, self.b],
            self.parts,
            after,
            carry,
            [pltpu.VMEM((self.rows // 2, self.mine.shape[1]), BF)],
        )
        self.parts = a, swap(a, 4), b, swap(b, 2)
        return a, *carry

    def join(self, after, carry=()):
        (a, b), carry = self.step(
            join_body, [2 * self.a, 2 * self.b], self.parts, after, carry
        )
        self.parts = a, swap(a, 2), b, swap(b, 4)
        return a, *carry

    def whole(self, after, carry=()):
        (x,), carry = self.step(whole_body, [2 * self.rows], self.parts, after, carry)
        return x, *carry


def place_rows(x, half, slab, out, wide, sems):
    count = x.shape[0] // 4
    rows = wide.shape[0] // 4
    copies = []
    for i in range(4):
        at = slice(i * rows, (i + 1) * rows)
        wide[at] = x[i * count : i * count + rows].astype(F32)
        to = pl.ds(pl.multiple_of(half * 4 * rows + i * rows, rows), rows)
        copies.append(pltpu.make_async_copy(wide.at[at], out.at[slab, to], sems.at[i]))
        copies[-1].start()
    return copies


def place_body(slab, flip, *refs):
    x, out, token, wide, sems = refs[0], refs[-4], refs[-3], refs[-2], refs[-1]
    copies = place_rows(x, (bit_of(1) + flip) % 2, slab, out, wide, sems)
    token[...] = jnp.zeros(token.shape, F32)
    for copy in copies:
        copy.wait()


def place(slab, flip, x, shape, held, after):
    hid = shape.shape[1]
    return call(
        functools.partial(place_body, slab, flip),
        (shape, Shape((8, 128), F32)),
        (x,) if held is None else (x, held),
        after,
        specs=[VMEM] if held is None else [VMEM, HBM],
        out_specs=(HBM, VMEM),
        scratch=[pltpu.VMEM((hid // 2, hid), F32), pltpu.SemaphoreType.DMA((4,))],
        aliases={} if held is None else {1: 0},
    )


def finish_body(
    n, x, got, held, out, lead_out, readout_out, own_out, wide, rest, lead, turned, sems
):
    hid = out.shape[1]
    levels = lead.shape[0] // 2
    bit = bit_of(1)
    quarter, part = hid // 8, rest.shape[0] // 8
    for ref, b in ((x, bit), (got, 1 - bit)):
        for i in range(4):
            at = pl.ds(pl.multiple_of(b * 4 * part + i * part, part), part)
            base = i * (quarter + part) + quarter
            rest[at] = ref[base : base + part].astype(F32)
    a = KEPT + n
    zeros = jnp.zeros((levels - KEPT, hid), F32)
    lead[: KEPT - 2] = rest[: KEPT - 2]
    lead[KEPT - 2 : levels] = jnp.zeros((levels - KEPT + 2, hid), F32)
    lead[levels : levels + KEPT] = rest[a : a + KEPT]
    lead[levels + KEPT :] = zeros
    copies = [pltpu.make_async_copy(lead, lead_out, sems.at[4])]
    copies[0].start()
    copies += place_rows(got, 1 - bit, 0, out, wide, sems)
    turned[...] = jnp.concatenate([rest[a + KEPT : a + 2 * KEPT], zeros], 0).T
    copies.append(pltpu.make_async_copy(turned, readout_out, sems.at[5]))
    copies[-1].start()
    own_out[...] = rest[pl.ds(KEPT + lax.axis_index("tiles"), 1)]
    for copy in copies:
        copy.wait()


def local(
    warmth,
    brine,
    flags,
    tally,
    assigned,
    desired,
    intercepts,
    leading,
    interior,
    readout,
):
    n = lax.axis_size("tiles")
    lon, lat, levels = warmth.shape
    cols = lon * lat
    hid = leading.shape[1]
    scale = 1.0 / math.sqrt(cols * n)

    wide = (lon, lat, levels)
    depth = jnp.where(flags > 0, tally, 0).astype(F32)
    depth = jnp.broadcast_to(depth[:, :, None], wide)
    owner = jnp.broadcast_to(assigned[:, :, None].astype(F32), wide)
    odd = bit_of(1) == 1
    first = jnp.stack([warmth[:1], brine[:1], depth[:1]])
    last = jnp.stack([warmth[-1:], brine[-1:], depth[-1:]])
    near = swap(jnp.where(odd, first, last), 1)
    pairs = [(t, (t + 1) % n if t % 2 else (t - 1) % n) for t in range(n)]
    far = lax.ppermute(jnp.where(odd, last, first), "tiles", pairs)
    bias = lax.all_to_all(
        jnp.broadcast_to(intercepts.reshape(1, hid // 128, 128), (n, hid // 128, 128)),
        "tiles",
        split_axis=0,
        concat_axis=0,
        tiled=True,
    )
    warmth, brine, desired, leading, interior, readout = [
        pltpu.with_memory_space_constraint(a, pltpu.HBM)
        for a in (warmth, brine, desired, leading, interior, readout)
    ]
    warmth, brine, desired = call(
        stage_body,
        [pltpu.VMEM(a.shape, a.dtype) for a in (warmth, brine, desired)],
        (warmth, brine, desired),
        specs=[HBM] * 3,
        scratch=[pltpu.SemaphoreType.DMA((3,))],
    )
    stepped, pack = call(
        step_body,
        (Shape((2,) + wide, F32), Shape((cols, 2 * levels), BF)),
        (depth, near, far, owner, warmth, brine, desired),
        bias,
    )
    pack_p = swap(pack, 4)
    act = Shape((cols, hid), BF)
    one = pltpu.VMEM(act.shape, BF)
    sem = pltpu.SemaphoreType.DMA((interior.shape[0] + 2,))
    trained = (act,) * 5 + (Shape(pack.shape, BF), Shape((KEPT, hid), F32))
    scratch = [pltpu.VMEM(interior.shape, BF), pltpu.VMEM(readout.shape, BF), one, one, sem]
    inferred, w_lead, act0, act1, slope0, slope1, delta2, feat, rest = call(
        functools.partial(forward_body, n, scale),
        (Shape(wide, BF), Shape(leading.shape, BF)) + trained,
        (pack, bias, leading, interior, readout),
        specs=[VMEM] * 2 + [HBM] * 3,
        scratch=scratch,
        room=ROOM,
    )
    half = Shape((hid // 4, hid), BF)
    act0_p, act1_p, slope0_p, slope1_p, delta2_p, feat_p, rest_p, other = call(
        functools.partial(partner_body, scale),
        trained + (half,),
        (pack_p, w_lead, interior, readout, act1, delta2),
        specs=[VMEM] * 2 + [HBM] * 2 + [VMEM] * 2,
        scratch=scratch,
        room=ROOM,
    )
    mine, delta1 = call(
        middle_body,
        (half, act),
        (interior, act1, delta2, act1_p, delta2_p, slope1),
        specs=[HBM] + [VMEM] * 5,
        scratch=[pltpu.VMEM((hid, hid), BF), sem],
        room=ROOM,
    )
    top = Sum(mine, [other], 1, 1, TOP_SHARE)
    (token,) = top.split(delta1)
    rows = rest_rows(n)
    part = Shape((hid // 4 + rows // 4, hid), BF)
    mine, *others = call(
        functools.partial(first_body, n),
        (part,) + (bf(part.shape[0] // 4, part),) * 4,
        (
            interior,
            feat,
            act0,
            slope0,
            delta1,
            rest,
            feat_p,
            act0_p,
            slope0_p,
            slope1_p,
            delta2_p,
            rest_p,
        ),
        token,
        specs=[HBM] + [VMEM] * 11,
        scratch=[
            *[one] * 3,
            pltpu.VMEM((rows, hid), BF),
            pltpu.VMEM(part.shape, BF),
            pltpu.VMEM(interior.shape, BF),
            sem,
        ],
        room=ROOM,
    )
    low = Sum(mine, others, 2, LOW_MIDS, LOW_SHARE)
    (token,) = top.pair(mine)
    (token,) = low.split(token)
    (token,) = top.unpair(token)
    (token,) = low.pair(token)
    (token,) = top.join(token)
    (token,) = low.unpair(token)
    (x,) = top.whole(token)
    grads = Shape((interior.shape[0], hid, hid), F32)
    token, x = low.join(None, [x])
    held, token = place(1, 0, x, grads, None, token)
    held, token = place(1, 1, swap(x, 1), grads, held, token)
    (y,) = low.whole(token)
    held, _ = place(0, 0, y, grads, held, None)
    interior_out, lead_out, readout_out, own_out = call(
        functools.partial(finish_body, n),
        (
            grads,
            Shape((2 * levels, hid), F32),
            Shape((hid, levels), F32),
            Shape((1, hid), F32),
        ),
        (y, swap(y, 1), held),
        specs=[VMEM, VMEM, HBM],
        out_specs=(HBM, HBM, HBM, VMEM),
        scratch=[
            pltpu.VMEM((hid // 2, hid), F32),
            pltpu.VMEM((rows, hid), F32),
            pltpu.VMEM((2 * levels, hid), F32),
            pltpu.VMEM((hid, levels), F32),
            pltpu.SemaphoreType.DMA((6,)),
        ],
        aliases={2: 0},
    )
    return stepped, inferred, lead_out, interior_out, readout_out, own_out


def solution(mesh):
    part = ("groups", "tiles")
    return jax.shard_map(
        local,
        mesh=mesh,
        in_specs=(
            P(part, None, None),
            P(part, None, None),
            P(part, None),
            P(part, None),
            P(part, None),
            P(part, None, None),
            P(part, None),
            P(),
            P(),
            P(),
        ),
        out_specs=(
            P(None, part, None, None),
            P(part, None, None),
            P("groups", None),
            P(None, "groups", None),
            P("groups", None),
            P(part, None),
        ),
        check_vma=False,
    )
```

```python
import functools
import math

import jax
import jax.numpy as jnp
from jax import lax
from jax.experimental import pallas as pl
from jax.experimental.pallas import tpu as pltpu
from jax.sharding import PartitionSpec as P

KAPPA = 0.2
KEPT = 80
PACKED = 48
BLOCK = 256
ROOM = 28
TOP_SHARE = 0.625
LOW_SHARE = 0.5
LOW_SENDS = 2
LOW_MIDS = 2
BF = jnp.bfloat16
F32 = jnp.float32
VMEM = pl.BlockSpec(memory_space=pltpu.VMEM)
ANY = pl.BlockSpec(memory_space=pl.ANY)
HBM = pl.BlockSpec(memory_space=pltpu.HBM)
Shape = jax.ShapeDtypeStruct


def contract_rows(left, right):
    return lax.dot_general(left, right, (((0,), (0,)), ((), ())), preferred_element_type=F32)


def times_transposed(left, right):
    return lax.dot_general(left, right, (((1,), (1,)), ((), ())), preferred_element_type=F32)


def bit_of(stride):
    return (lax.axis_index("tiles") // stride) % 2


def rows_at(index, rows):
    return pl.ds(pl.multiple_of(index * rows, rows), rows)


def rest_rows(n):
    return -(-(n + 3 * KEPT) // 256) * 256


def call(
    body, outs, args, after=None, carry=(), specs=None, out_specs=None, scratch=(), aliases=None, room=12
):
    outs, args = tuple(outs), tuple(args)
    specs = list(specs or [VMEM] * len(args))
    out_specs = list(out_specs or [VMEM] * len(outs))
    count, made = len(args), len(outs)
    aliases = dict(aliases or {})
    extra = (() if after is None else (after,)) + tuple(carry)
    for i, array in enumerate(carry):
        aliases[count + len(extra) - len(carry) + i] = made + i
    plain = body

    def body(*refs):
        given = refs[:count]
        rest = refs[count + len(extra) :]
        plain(*given, *rest[:made], *rest[made + len(carry) :])

    return pl.pallas_call(
        body,
        out_shape=outs + tuple(Shape(a.shape, a.dtype) for a in carry),
        in_specs=specs + [ANY] * len(extra),
        out_specs=tuple(out_specs + [ANY] * len(carry)),
        scratch_shapes=scratch,
        input_output_aliases=aliases,
        compiler_params=pltpu.CompilerParams(vmem_limit_bytes=room * 2**20),
        cost_estimate=pl.CostEstimate(flops=1, bytes_accessed=1, transcendentals=0),
    )(*args, *extra)


def activate(v):
    s = 0.5 + 0.5 * jnp.tanh(0.5 * v)
    act = (v * s).astype(BF)
    s = s.astype(BF)
    return act, s + act * (1.0 - s)


def stage_body(*refs):
    count = len(refs) // 2
    copies = [
        pltpu.make_async_copy(refs[i], refs[count + i], refs[-1].at[i]) for i in range(count)
    ]
    for copy in copies:
        copy.start()
    for copy in copies:
        copy.wait()


def step_body(depth, near, far, owner, warm, brine, desired, stepped, pack):
    lon, lat, levels = warm.shape
    cols = lon * lat
    odd = bit_of(1) == 1
    before = jnp.where(odd, near[...], far[...])
    after = jnp.where(odd, far[...], near[...])
    level = lax.broadcasted_iota(jnp.int32, (lon, lat, levels), 2).astype(F32)
    row = lax.broadcasted_iota(jnp.int32, (lon, lat, levels), 1)
    wet = (level < depth[...]).astype(F32)
    wet_b = (level[:1] < before[2]).astype(F32)
    wet_a = (level[:1] < after[2]).astype(F32)
    wet_e = jnp.concatenate([wet[1:], wet_a], 0)
    wet_w = jnp.concatenate([wet_b, wet[:-1]], 0)
    wet_n = jnp.where(row < lat - 1, pltpu.roll(wet, lat - 1, 1), 0.0)
    wet_s = jnp.where(row > 0, pltpu.roll(wet, 1, 1), 0.0)
    lane = lax.broadcasted_iota(jnp.int32, (cols, levels), 1)
    target = desired[...].reshape(cols, levels).astype(F32)
    for i, ref in enumerate((warm, brine)):
        q = ref[...]
        total = wet_e * (jnp.concatenate([q[1:], after[i]], 0) - q)
        total = total + wet_w * (jnp.concatenate([before[i], q[:-1]], 0) - q)
        total = total + wet_n * (pltpu.roll(q, lat - 1, 1) - q)
        total = total + wet_s * (pltpu.roll(q, 1, 1) - q)
        out = q + KAPPA * wet * total
        stepped[i] = out
        group = (out * wet).reshape(cols, levels)
        if i == 0:
            group = jnp.where(lane == KEPT - 2, owner[...].reshape(cols, levels), group)
            group = jnp.where(lane == KEPT - 1, depth[...].reshape(cols, levels), group)
        beside = pltpu.roll(target, (KEPT - i * PACKED) % levels, 1)
        group = jnp.where(lane >= KEPT, beside, group)
        pack[:, i * levels : (i + 1) * levels] = group.astype(BF)


def weight_grad(pairs, at):
    total = None
    for act, delta in pairs:
        term = contract_rows(act[:, at], delta[...])
        total = term if total is None else total + term
    return total.astype(BF)


def back_through(delta, weights, slope, out):
    for j in range(0, out.shape[1], BLOCK):
        back = times_transposed(delta, weights[j : j + BLOCK])
        out[:, j : j + BLOCK] = (back * slope[:, j : j + BLOCK].astype(F32)).astype(BF)


def train(scale, pack, interior, readout, inferred, outs, scratch, weights):
    act0, act1, slope0, slope1, delta2, feat, rest = outs
    w_int, w_out, act2, slope2, sems = scratch
    cols = pack.shape[0]
    levels = pack.shape[1] // 2
    hid = readout.shape[0]
    deep = interior.shape[0]
    start_weights, w_lead = weights
    start_weights()
    copies = [
        pltpu.make_async_copy(interior.at[i], w_int.at[i], sems.at[i]) for i in range(deep)
    ]
    copies.append(pltpu.make_async_copy(readout, w_out, sems.at[deep]))
    for copy in copies:
        copy.start()
    groups = [pack[:, i * levels : (i + 1) * levels].astype(F32) for i in range(2)]
    lane = lax.broadcasted_iota(jnp.int32, (cols, levels), 1)
    own = lane.astype(F32) == groups[0][:, KEPT - 2 : KEPT - 1] + KEPT
    wet = lane.astype(F32) < groups[0][:, KEPT - 1 : KEPT]
    target = jnp.where(
        lane < PACKED,
        pltpu.roll(groups[0], levels - KEPT, 1),
        pltpu.roll(groups[1], levels - KEPT + PACKED, 1),
    )
    for i, group in enumerate(groups):
        hot = jnp.where(own, 1.0, 0.0)
        feat[:, i * levels : (i + 1) * levels] = jnp.where(lane < KEPT - 2, group, hot).astype(BF)
    w_lead = w_lead()
    for layer, (left, right, act, slope) in enumerate(
        (
            (feat, w_lead, act0, slope0),
            (act0, w_int.at[0], act1, slope1),
            (act1, w_int.at[1], act2, slope2),
        )
    ):
        if layer:
            copies[layer - 1].wait()
        for j in range(0, hid, BLOCK):
            pre = jnp.dot(left[...], right[:, j : j + BLOCK], preferred_element_type=F32)
            act[:, j : j + BLOCK], slope[:, j : j + BLOCK] = activate(pre)
    copies[deep].wait()
    output = jnp.dot(act2[...], w_out[...], preferred_element_type=F32)
    if inferred is not None:
        inferred[...] = output.astype(BF).reshape(inferred.shape)
    err = jnp.where(wet, (output - target) * scale, 0.0).astype(BF)
    back_through(err, w_out, slope2, delta2)
    rest[...] = contract_rows(err, act2[...])[:KEPT]


def forward_body(n, scale, pack, bias, leading, interior, readout, *refs):
    inferred, w_lead, refs = refs[0], refs[1], refs[2:]
    copy = pltpu.make_async_copy(leading, w_lead, refs[-1].at[interior.shape[0] + 1])

    def weights():
        copy.wait()
        for j in range(bias.shape[1]):
            value = bias[:, j]
            high = value.astype(BF)
            at = slice(j * bias.shape[2], (j + 1) * bias.shape[2])
            low = (value - high.astype(F32)).astype(BF)
            w_lead[KEPT : KEPT + n, at] = high
            w_lead[bias.shape[2] + KEPT : bias.shape[2] + KEPT + n, at] = low
        return w_lead

    train(scale, pack, interior, readout, inferred, refs[:7], refs[7:], (copy.start, weights))


def partner_body(
    scale, pack, w_lead, interior, readout, act1, delta2, *refs
):
    outs, other, scratch = refs[:7], refs[7], refs[8:]
    train(
        scale, pack, interior, readout, None, outs, scratch, (lambda: None, lambda: w_lead)
    )
    rows = other.shape[0]
    at = pl.ds(pl.multiple_of((1 - bit_of(1)) * 2 * rows + bit_of(4) * rows, rows), rows)
    other[...] = weight_grad(((act1, delta2), (outs[1], outs[4])), at)


def middle_body(
    interior, act1, delta2, act1_p, delta2_p, slope1, mine, delta1, w_int, sems
):
    copy = pltpu.make_async_copy(interior.at[1], w_int, sems.at[0])
    copy.start()
    rows = mine.shape[0]
    at = pl.ds(pl.multiple_of(bit_of(1) * 2 * rows + bit_of(4) * rows, rows), rows)
    mine[...] = weight_grad(((act1, delta2), (act1_p, delta2_p)), at)
    copy.wait()
    back_through(delta2[...], w_int, slope1, delta1)


def first_body(
    n,
    interior,
    feat,
    act0,
    slope0,
    delta1,
    rest_in,
    feat_p,
    act0_p,
    slope0_p,
    slope1_p,
    delta2_p,
    rest_p,
    mine,
    other_0,
    other_1,
    other_2,
    other_3,
    delta1_p,
    delta0,
    delta0_p,
    rest,
    spare,
    w_int,
    sems,
):
    levels = feat.shape[1] // 2
    hid = slope0.shape[1]
    copies = [
        pltpu.make_async_copy(interior.at[i], w_int.at[i], sems.at[i])
        for i in range(interior.shape[0])
    ]
    for copy in reversed(copies):
        copy.start()
    copies[1].wait()
    back_through(delta2_p[...], w_int.at[1], slope1_p, delta1_p)
    copies[0].wait()
    back_through(delta1[...], w_int.at[0], slope0, delta0)
    back_through(delta1_p[...], w_int.at[0], slope0_p, delta0_p)
    total = contract_rows(feat[...], delta0[...]) + contract_rows(feat_p[...], delta0_p[...])
    lead = total.astype(BF)
    a = KEPT + n
    rest[:a] = lead[:a]
    rest[a : a + KEPT] = lead[levels : levels + KEPT]
    rest[a + KEPT : a + 2 * KEPT] = (rest_in[...] + rest_p[...]).astype(BF)
    rows = rest.shape[0]
    if rows > a + 2 * KEPT:
        rest[a + 2 * KEPT :] = jnp.zeros((rows - a - 2 * KEPT, hid), BF)
    bit, z = bit_of(1), bit_of(4)
    quarter, part = hid // 8, rows // 8
    for ref, b in ((spare, 1 - bit), (mine, bit)):
        at = pl.ds(pl.multiple_of((b * 2 + z) * 2 * quarter, 2 * quarter), 2 * quarter)
        got = weight_grad(((act0, delta1), (act0_p, delta1_p)), at)
        for y in range(2):
            base = y * (quarter + part)
            ref[base : base + quarter] = got[y * quarter : (y + 1) * quarter]
            from_rest = pl.ds(pl.multiple_of((b * 2 + z) * 2 * part + y * part, part), part)
            ref[base + quarter : base + quarter + part] = rest[from_rest]
    for i, ref in enumerate((other_0, other_1, other_2, other_3)):
        ref[...] = spare[i * ref.shape[0] : (i + 1) * ref.shape[0]]


def split_body(count, mine, *refs):
    got, keep, sends, total = refs[:count], refs[count], refs[count + 1 : -1], refs[-1]
    base = 0
    for ref in got:
        at = slice(base, base + ref.shape[0])
        total[at] = mine[at] + ref[...]
        base += ref.shape[0]
    bit = bit_of(2)
    rows = keep.shape[0]
    keep[...] = total[rows_at(bit, rows)]
    for i, send in enumerate(sends):
        part = send.shape[0]
        at = pl.ds(pl.multiple_of((1 - bit) * rows + i * part, 16), part)
        send[...] = total[at]


def rows_of(refs):
    base, places = 0, []
    for ref in refs:
        places.append(slice(base, base + ref.shape[0]))
        base += ref.shape[0]
    return places


def pair_body(count, keep, *refs):
    got, outs, total = refs[:count], refs[count:-1], refs[-1]
    for ref, at in zip(got, rows_of(got)):
        total[at] = keep[at] + ref[...]
    for ref, at in zip(outs, rows_of(outs)):
        ref[...] = total[at]


def unpair_body(count, *refs):
    own, got, (a, b, total) = refs[:count], refs[count : 2 * count], refs[2 * count :]
    for x, ref, at in zip(own, got, rows_of(own)):
        total[at] = x[...] + ref[...]
    for ref, at in zip((a, b), rows_of((a, b))):
        ref[...] = total[at]


def join_body(a, got_a, b, got_b, a_out, b_out):
    for stride, x, got, out in ((4, a, got_a, a_out), (2, b, got_b, b_out)):
        bit = bit_of(stride)
        rows = x.shape[0]
        out[rows_at(bit, rows)] = x[...]
        out[rows_at(1 - bit, rows)] = got[...]


def whole_body(a, got_a, b, got_b, out):
    rows = a.shape[0] // 2, b.shape[0] // 2
    y, z = bit_of(2), bit_of(4)

    def at(z, y, low):
        base = (z * 2 + y) * (rows[0] + rows[1]) + low * rows[0]
        return pl.ds(pl.multiple_of(base, 16), rows[low])

    for i in range(2):
        own = slice(i * rows[0], (i + 1) * rows[0])
        out[at(i, y, 0)] = a[own]
        out[at(i, 1 - y, 0)] = got_a[own]
        own = slice(i * rows[1], (i + 1) * rows[1])
        out[at(z, i, 1)] = b[own]
        out[at(1 - z, i, 1)] = got_b[own]


def swap(x, stride):
    n = lax.axis_size("tiles")
    return lax.ppermute(x, "tiles", [(t, t ^ stride) for t in range(n)])


def bf(rows, like):
    return Shape((rows, like.shape[1]), BF)


class Sum:
    def __init__(self, mine, others, sends, mids, share):
        self.mine, self.got = mine, [swap(other, 1) for other in others]
        self.rows, self.sends, self.mids = mine.shape[0], sends, mids
        self.a = int(share * self.rows / 32) * 16
        self.b = self.rows // 2 - self.a

    def step(self, body, rows, args, after, carry=(), scratch=()):
        outs = [bf(r, self.mine) for r in rows]
        made = call(body, outs, args, after, carry, scratch=scratch)
        return made[: len(rows)], made[len(rows) :]

    def split(self, after, carry=()):
        half = self.rows // 2
        (keep, *sends), carry = self.step(
            functools.partial(split_body, len(self.got)),
            [half] + [half // self.sends] * self.sends,
            (self.mine, *self.got),
            after,
            carry,
            [pltpu.VMEM(self.mine.shape, BF)],
        )
        self.parts = (keep, *[swap(send, 2) for send in sends])
        return keep, *carry

    def pair(self, after, carry=()):
        half = self.rows // 2
        m, carry = self.step(
            functools.partial(pair_body, len(self.parts) - 1),
            [half // self.mids] * self.mids,
            self.parts,
            after,
            carry,
            [pltpu.VMEM((half, self.mine.shape[1]), BF)],
        )
        token, stride = m[0], 8
        while 2 * stride < lax.axis_size("tiles"):
            m = [x + swap(x, stride) for x in m]
            stride *= 2
        self.parts = (*m, *[swap(x, stride) for x in m])
        return token, *carry

    def unpair(self, after, carry=()):
        (a, b), carry = self.step(
            functools.partial(unpair_body, self.mids),
            [self.a, self.b],
            self.parts,
            after,
            carry,
            [pltpu.VMEM((self.rows // 2, self.mine.shape[1]), BF)],
        )
        self.parts = a, swap(a, 4), b, swap(b, 2)
        return a, *carry

    def join(self, after, carry=()):
        (a, b), carry = self.step(
            join_body, [2 * self.a, 2 * self.b], self.parts, after, carry
        )
        self.parts = a, swap(a, 2), b, swap(b, 4)
        return a, *carry

    def whole(self, after, carry=()):
        (x,), carry = self.step(whole_body, [2 * self.rows], self.parts, after, carry)
        return x, *carry


def place_rows(x, half, slab, out, wide, sems):
    count = x.shape[0] // 4
    rows = wide.shape[0] // 4
    copies = []
    for i in range(4):
        at = slice(i * rows, (i + 1) * rows)
        wide[at] = x[i * count : i * count + rows].astype(F32)
        to = pl.ds(pl.multiple_of(half * 4 * rows + i * rows, rows), rows)
        copies.append(pltpu.make_async_copy(wide.at[at], out.at[slab, to], sems.at[i]))
        copies[-1].start()
    return copies


def place_body(slab, flip, *refs):
    x, out, token, wide, sems = refs[0], refs[-4], refs[-3], refs[-2], refs[-1]
    copies = place_rows(x, (bit_of(1) + flip) % 2, slab, out, wide, sems)
    token[...] = jnp.zeros(token.shape, F32)
    for copy in copies:
        copy.wait()


def place(slab, flip, x, shape, held, after):
    hid = shape.shape[1]
    return call(
        functools.partial(place_body, slab, flip),
        (shape, Shape((8, 128), F32)),
        (x,) if held is None else (x, held),
        after,
        specs=[VMEM] if held is None else [VMEM, HBM],
        out_specs=(HBM, VMEM),
        scratch=[pltpu.VMEM((hid // 2, hid), F32), pltpu.SemaphoreType.DMA((4,))],
        aliases={} if held is None else {1: 0},
    )


def finish_body(
    n, x, got, held, out, lead_out, readout_out, own_out, wide, rest, lead, turned, sems
):
    hid = out.shape[1]
    levels = lead.shape[0] // 2
    bit = bit_of(1)
    quarter, part = hid // 8, rest.shape[0] // 8
    for ref, b in ((x, bit), (got, 1 - bit)):
        for i in range(4):
            at = pl.ds(pl.multiple_of(b * 4 * part + i * part, part), part)
            base = i * (quarter + part) + quarter
            rest[at] = ref[base : base + part].astype(F32)
    a = KEPT + n
    zeros = jnp.zeros((levels - KEPT, hid), F32)
    turned[...] = jnp.concatenate([rest[a + KEPT : a + 2 * KEPT], zeros], 0).T
    copies = [pltpu.make_async_copy(turned, readout_out, sems.at[5])]
    copies[0].start()
    lead[: KEPT - 2] = rest[: KEPT - 2]
    lead[KEPT - 2 : levels] = jnp.zeros((levels - KEPT + 2, hid), F32)
    lead[levels : levels + KEPT] = rest[a : a + KEPT]
    lead[levels + KEPT :] = zeros
    copies.append(pltpu.make_async_copy(lead, lead_out, sems.at[4]))
    copies[-1].start()
    copies += place_rows(got, 1 - bit, 0, out, wide, sems)
    own_out[...] = rest[pl.ds(KEPT + lax.axis_index("tiles"), 1)]
    for copy in copies:
        copy.wait()


def local(
    warmth,
    brine,
    flags,
    tally,
    assigned,
    desired,
    intercepts,
    leading,
    interior,
    readout,
):
    n = lax.axis_size("tiles")
    lon, lat, levels = warmth.shape
    cols = lon * lat
    hid = leading.shape[1]
    scale = 1.0 / math.sqrt(cols * n)

    wide = (lon, lat, levels)
    depth = jnp.where(flags > 0, tally, 0).astype(F32)
    depth = jnp.broadcast_to(depth[:, :, None], wide)
    owner = jnp.broadcast_to(assigned[:, :, None].astype(F32), wide)
    odd = bit_of(1) == 1
    first = jnp.stack([warmth[:1], brine[:1], depth[:1]])
    last = jnp.stack([warmth[-1:], brine[-1:], depth[-1:]])
    near = swap(jnp.where(odd, first, last), 1)
    pairs = [(t, (t + 1) % n if t % 2 else (t - 1) % n) for t in range(n)]
    far = lax.ppermute(jnp.where(odd, last, first), "tiles", pairs)
    bias = lax.all_to_all(
        jnp.broadcast_to(intercepts.reshape(1, hid // 128, 128), (n, hid // 128, 128)),
        "tiles",
        split_axis=0,
        concat_axis=0,
        tiled=True,
    )
    warmth, brine, desired, leading, interior, readout = [
        pltpu.with_memory_space_constraint(a, pltpu.HBM)
        for a in (warmth, brine, desired, leading, interior, readout)
    ]
    warmth, brine, desired = call(
        stage_body,
        [pltpu.VMEM(a.shape, a.dtype) for a in (warmth, brine, desired)],
        (warmth, brine, desired),
        specs=[HBM] * 3,
        scratch=[pltpu.SemaphoreType.DMA((3,))],
    )
    stepped, pack = call(
        step_body,
        (Shape((2,) + wide, F32), Shape((cols, 2 * levels), BF)),
        (depth, near, far, owner, warmth, brine, desired),
        bias,
    )
    pack_p = swap(pack, 4)
    act = Shape((cols, hid), BF)
    one = pltpu.VMEM(act.shape, BF)
    sem = pltpu.SemaphoreType.DMA((interior.shape[0] + 2,))
    trained = (act,) * 5 + (Shape(pack.shape, BF), Shape((KEPT, hid), F32))
    scratch = [pltpu.VMEM(interior.shape, BF), pltpu.VMEM(readout.shape, BF), one, one, sem]
    inferred, w_lead, act0, act1, slope0, slope1, delta2, feat, rest = call(
        functools.partial(forward_body, n, scale),
        (Shape(wide, BF), Shape(leading.shape, BF)) + trained,
        (pack, bias, leading, interior, readout),
        specs=[VMEM] * 2 + [HBM] * 3,
        scratch=scratch,
        room=ROOM,
    )
    half = Shape((hid // 4, hid), BF)
    act0_p, act1_p, slope0_p, slope1_p, delta2_p, feat_p, rest_p, other = call(
        functools.partial(partner_body, scale),
        trained + (half,),
        (pack_p, w_lead, interior, readout, act1, delta2),
        specs=[VMEM] * 2 + [HBM] * 2 + [VMEM] * 2,
        scratch=scratch,
        room=ROOM,
    )
    mine, delta1 = call(
        middle_body,
        (half, act),
        (interior, act1, delta2, act1_p, delta2_p, slope1),
        specs=[HBM] + [VMEM] * 5,
        scratch=[pltpu.VMEM((hid, hid), BF), sem],
        room=ROOM,
    )
    top = Sum(mine, [other], 1, 1, TOP_SHARE)
    (token,) = top.split(delta1)
    rows = rest_rows(n)
    part = Shape((hid // 4 + rows // 4, hid), BF)
    mine, *others = call(
        functools.partial(first_body, n),
        (part,) + (bf(part.shape[0] // 4, part),) * 4,
        (
            interior,
            feat,
            act0,
            slope0,
            delta1,
            rest,
            feat_p,
            act0_p,
            slope0_p,
            slope1_p,
            delta2_p,
            rest_p,
        ),
        token,
        specs=[HBM] + [VMEM] * 11,
        scratch=[
            *[one] * 3,
            pltpu.VMEM((rows, hid), BF),
            pltpu.VMEM(part.shape, BF),
            pltpu.VMEM(interior.shape, BF),
            sem,
        ],
        room=ROOM,
    )
    low = Sum(mine, others, LOW_SENDS, LOW_MIDS, LOW_SHARE)
    (token,) = top.pair(mine)
    (token,) = low.split(token)
    (token,) = top.unpair(token)
    (token,) = low.pair(token)
    (token,) = top.join(token)
    (token,) = low.unpair(token)
    (x,) = top.whole(token)
    grads = Shape((interior.shape[0], hid, hid), F32)
    token, x = low.join(None, [x])
    held, token = place(1, 0, x, grads, None, token)
    held, token = place(1, 1, swap(x, 1), grads, held, token)
    (y,) = low.whole(token)
    held, _ = place(0, 0, y, grads, held, None)
    interior_out, lead_out, readout_out, own_out = call(
        functools.partial(finish_body, n),
        (
            grads,
            Shape((2 * levels, hid), F32),
            Shape((hid, levels), F32),
            Shape((1, hid), F32),
        ),
        (y, swap(y, 1), held),
        specs=[VMEM, VMEM, HBM],
        out_specs=(HBM, HBM, HBM, VMEM),
        scratch=[
            pltpu.VMEM((hid // 2, hid), F32),
            pltpu.VMEM((rows, hid), F32),
            pltpu.VMEM((2 * levels, hid), F32),
            pltpu.VMEM((hid, levels), F32),
            pltpu.SemaphoreType.DMA((6,)),
        ],
        aliases={2: 0},
    )
    return stepped, inferred, lead_out, interior_out, readout_out, own_out


def solution(mesh):
    part = ("groups", "tiles")
    return jax.shard_map(
        local,
        mesh=mesh,
        in_specs=(
            P(part, None, None),
            P(part, None, None),
            P(part, None),
            P(part, None),
            P(part, None),
            P(part, None, None),
            P(part, None),
            P(),
            P(),
            P(),
        ),
        out_specs=(
            P(None, part, None, None),
            P(part, None, None),
            P("groups", None),
            P(None, "groups", None),
            P("groups", None),
            P(part, None),
        ),
        check_vma=False,
    )
```

```python
import functools
import math

import jax
import jax.numpy as jnp
from jax import lax
from jax.experimental import pallas as pl
from jax.experimental.pallas import tpu as pltpu
from jax.sharding import PartitionSpec as P

KAPPA = 0.2
KEPT = 80
PACKED = 48
BLOCK = 256
ROOM = 28
TOP_SHARE = 0.625
LOW_SHARE = 0.5
LOW_SENDS = 2
LOW_MIDS = 2
BF = jnp.bfloat16
F32 = jnp.float32
VMEM = pl.BlockSpec(memory_space=pltpu.VMEM)
ANY = pl.BlockSpec(memory_space=pl.ANY)
HBM = pl.BlockSpec(memory_space=pltpu.HBM)
Shape = jax.ShapeDtypeStruct


def contract_rows(left, right):
    return lax.dot_general(left, right, (((0,), (0,)), ((), ())), preferred_element_type=F32)


def times_transposed(left, right):
    return lax.dot_general(left, right, (((1,), (1,)), ((), ())), preferred_element_type=F32)


def bit_of(stride):
    return (lax.axis_index("tiles") // stride) % 2


def rows_at(index, rows):
    return pl.ds(pl.multiple_of(index * rows, rows), rows)


def rest_rows(n):
    return -(-(n + 3 * KEPT) // 256) * 256


def call(
    body, outs, args, after=None, carry=(), specs=None, out_specs=None, scratch=(), aliases=None, room=12
):
    outs, args = tuple(outs), tuple(args)
    specs = list(specs or [VMEM] * len(args))
    out_specs = list(out_specs or [VMEM] * len(outs))
    count, made = len(args), len(outs)
    aliases = dict(aliases or {})
    extra = (() if after is None else (after,)) + tuple(carry)
    for i, array in enumerate(carry):
        aliases[count + len(extra) - len(carry) + i] = made + i
    plain = body

    def body(*refs):
        given = refs[:count]
        rest = refs[count + len(extra) :]
        plain(*given, *rest[:made], *rest[made + len(carry) :])

    return pl.pallas_call(
        body,
        out_shape=outs + tuple(Shape(a.shape, a.dtype) for a in carry),
        in_specs=specs + [ANY] * len(extra),
        out_specs=tuple(out_specs + [ANY] * len(carry)),
        scratch_shapes=scratch,
        input_output_aliases=aliases,
        compiler_params=pltpu.CompilerParams(vmem_limit_bytes=room * 2**20),
        cost_estimate=pl.CostEstimate(flops=1, bytes_accessed=1, transcendentals=0),
    )(*args, *extra)


def activate(v):
    s = 0.5 + 0.5 * jnp.tanh(0.5 * v)
    act = (v * s).astype(BF)
    s = s.astype(BF)
    return act, s + act * (1.0 - s)


def stage_body(*refs):
    count = len(refs) // 2
    copies = [
        pltpu.make_async_copy(refs[i], refs[count + i], refs[-1].at[i]) for i in range(count)
    ]
    for copy in copies:
        copy.start()
    for copy in copies:
        copy.wait()


def step_body(depth, near, far, owner, warm, brine, desired, stepped, pack):
    lon, lat, levels = warm.shape
    cols = lon * lat
    odd = bit_of(1) == 1
    before = jnp.where(odd, near[...], far[...])
    after = jnp.where(odd, far[...], near[...])
    level = lax.broadcasted_iota(jnp.int32, (lon, lat, levels), 2).astype(F32)
    row = lax.broadcasted_iota(jnp.int32, (lon, lat, levels), 1)
    wet = (level < depth[...]).astype(F32)
    wet_b = (level[:1] < before[2]).astype(F32)
    wet_a = (level[:1] < after[2]).astype(F32)
    wet_e = jnp.concatenate([wet[1:], wet_a], 0)
    wet_w = jnp.concatenate([wet_b, wet[:-1]], 0)
    wet_n = jnp.where(row < lat - 1, pltpu.roll(wet, lat - 1, 1), 0.0)
    wet_s = jnp.where(row > 0, pltpu.roll(wet, 1, 1), 0.0)
    lane = lax.broadcasted_iota(jnp.int32, (cols, levels), 1)
    target = desired[...].reshape(cols, levels).astype(F32)
    for i, ref in enumerate((warm, brine)):
        q = ref[...]
        total = wet_e * (jnp.concatenate([q[1:], after[i]], 0) - q)
        total = total + wet_w * (jnp.concatenate([before[i], q[:-1]], 0) - q)
        total = total + wet_n * (pltpu.roll(q, lat - 1, 1) - q)
        total = total + wet_s * (pltpu.roll(q, 1, 1) - q)
        out = q + KAPPA * wet * total
        stepped[i] = out
        group = (out * wet).reshape(cols, levels)
        if i == 0:
            group = jnp.where(lane == KEPT - 2, owner[...].reshape(cols, levels), group)
            group = jnp.where(lane == KEPT - 1, depth[...].reshape(cols, levels), group)
        beside = pltpu.roll(target, (KEPT - i * PACKED) % levels, 1)
        group = jnp.where(lane >= KEPT, beside, group)
        pack[:, i * levels : (i + 1) * levels] = group.astype(BF)


def weight_grad(pairs, at):
    total = None
    for act, delta in pairs:
        term = contract_rows(act[:, at], delta[...])
        total = term if total is None else total + term
    return total.astype(BF)


def back_through(delta, weights, slope, out, start=0, stop=None):
    for j in range(start, stop or out.shape[1], BLOCK):
        back = times_transposed(delta, weights[j : j + BLOCK])
        out[:, j : j + BLOCK] = (back * slope[:, j : j + BLOCK].astype(F32)).astype(BF)


def train(scale, pack, interior, readout, inferred, outs, scratch, weights):
    act0, act1, slope0, slope1, delta2, feat, rest = outs
    w_int, w_out, act2, slope2, sems = scratch
    cols = pack.shape[0]
    levels = pack.shape[1] // 2
    hid = readout.shape[0]
    deep = interior.shape[0]
    start_weights, w_lead = weights
    start_weights()
    copies = [
        pltpu.make_async_copy(interior.at[i], w_int.at[i], sems.at[i]) for i in range(deep)
    ]
    copies.append(pltpu.make_async_copy(readout, w_out, sems.at[deep]))
    for copy in copies:
        copy.start()
    groups = [pack[:, i * levels : (i + 1) * levels].astype(F32) for i in range(2)]
    lane = lax.broadcasted_iota(jnp.int32, (cols, levels), 1)
    own = lane.astype(F32) == groups[0][:, KEPT - 2 : KEPT - 1] + KEPT
    wet = lane.astype(F32) < groups[0][:, KEPT - 1 : KEPT]
    target = jnp.where(
        lane < PACKED,
        pltpu.roll(groups[0], levels - KEPT, 1),
        pltpu.roll(groups[1], levels - KEPT + PACKED, 1),
    )
    for i, group in enumerate(groups):
        hot = jnp.where(own, 1.0, 0.0)
        feat[:, i * levels : (i + 1) * levels] = jnp.where(lane < KEPT - 2, group, hot).astype(BF)
    w_lead = w_lead()
    for layer, (left, right, act, slope) in enumerate(
        (
            (feat, w_lead, act0, slope0),
            (act0, w_int.at[0], act1, slope1),
            (act1, w_int.at[1], act2, slope2),
        )
    ):
        if layer:
            copies[layer - 1].wait()
        for j in range(0, hid, BLOCK):
            pre = jnp.dot(left[...], right[:, j : j + BLOCK], preferred_element_type=F32)
            act[:, j : j + BLOCK], slope[:, j : j + BLOCK] = activate(pre)
    copies[deep].wait()
    output = jnp.dot(act2[...], w_out[...], preferred_element_type=F32)
    if inferred is not None:
        inferred[...] = output.astype(BF).reshape(inferred.shape)
    err = jnp.where(wet, (output - target) * scale, 0.0).astype(BF)
    back_through(err, w_out, slope2, delta2)
    rest[...] = contract_rows(err, act2[...])[:KEPT]


def forward_body(n, scale, pack, bias, leading, interior, readout, *refs):
    inferred, w_lead, refs = refs[0], refs[1], refs[2:]
    copy = pltpu.make_async_copy(leading, w_lead, refs[-1].at[interior.shape[0] + 1])

    def weights():
        copy.wait()
        for j in range(bias.shape[1]):
            value = bias[:, j]
            high = value.astype(BF)
            at = slice(j * bias.shape[2], (j + 1) * bias.shape[2])
            low = (value - high.astype(F32)).astype(BF)
            w_lead[KEPT : KEPT + n, at] = high
            w_lead[bias.shape[2] + KEPT : bias.shape[2] + KEPT + n, at] = low
        return w_lead

    train(scale, pack, interior, readout, inferred, refs[:7], refs[7:], (copy.start, weights))


def partner_body(
    scale, pack, w_lead, interior, readout, act1, delta2, *refs
):
    outs, other, scratch = refs[:7], refs[7], refs[8:]
    train(
        scale, pack, interior, readout, None, outs, scratch, (lambda: None, lambda: w_lead)
    )
    rows = other.shape[0]
    at = pl.ds(pl.multiple_of((1 - bit_of(1)) * 2 * rows + bit_of(4) * rows, rows), rows)
    other[...] = weight_grad(((act1, delta2), (outs[1], outs[4])), at)


def middle_body(interior, act1, delta2, act1_p, delta2_p, slope1, mine, low, w_int, sems):
    units = low.shape[1]
    copy = pltpu.make_async_copy(interior.at[1, pl.ds(0, units)], w_int, sems.at[0])
    copy.start()
    rows = mine.shape[0]
    at = pl.ds(pl.multiple_of(bit_of(1) * 2 * rows + bit_of(4) * rows, rows), rows)
    mine[...] = weight_grad(((act1, delta2), (act1_p, delta2_p)), at)
    copy.wait()
    back_through(delta2[...], w_int, slope1, low)


def first_body(
    n,
    interior,
    feat,
    act0,
    slope0,
    slope1,
    delta2,
    low,
    rest_in,
    feat_p,
    act0_p,
    slope0_p,
    slope1_p,
    delta2_p,
    rest_p,
    mine,
    other_0,
    other_1,
    other_2,
    other_3,
    delta1,
    delta1_p,
    delta0,
    delta0_p,
    rest,
    spare,
    w_int,
    sems,
):
    levels = feat.shape[1] // 2
    hid = slope0.shape[1]
    copies = [
        pltpu.make_async_copy(interior.at[i], w_int.at[i], sems.at[i])
        for i in range(interior.shape[0])
    ]
    for copy in reversed(copies):
        copy.start()
    units = low.shape[1]
    delta1[:, :units] = low[...]
    copies[1].wait()
    back_through(delta2[...], w_int.at[1], slope1, delta1, units)
    back_through(delta2_p[...], w_int.at[1], slope1_p, delta1_p)
    copies[0].wait()
    back_through(delta1[...], w_int.at[0], slope0, delta0)
    back_through(delta1_p[...], w_int.at[0], slope0_p, delta0_p)
    total = contract_rows(feat[...], delta0[...]) + contract_rows(feat_p[...], delta0_p[...])
    lead = total.astype(BF)
    a = KEPT + n
    rest[:a] = lead[:a]
    rest[a : a + KEPT] = lead[levels : levels + KEPT]
    rest[a + KEPT : a + 2 * KEPT] = (rest_in[...] + rest_p[...]).astype(BF)
    rows = rest.shape[0]
    if rows > a + 2 * KEPT:
        rest[a + 2 * KEPT :] = jnp.zeros((rows - a - 2 * KEPT, hid), BF)
    bit, z = bit_of(1), bit_of(4)
    quarter, part = hid // 8, rows // 8
    for ref, b in ((spare, 1 - bit), (mine, bit)):
        at = pl.ds(pl.multiple_of((b * 2 + z) * 2 * quarter, 2 * quarter), 2 * quarter)
        got = weight_grad(((act0, delta1), (act0_p, delta1_p)), at)
        for y in range(2):
            base = y * (quarter + part)
            ref[base : base + quarter] = got[y * quarter : (y + 1) * quarter]
            from_rest = pl.ds(pl.multiple_of((b * 2 + z) * 2 * part + y * part, part), part)
            ref[base + quarter : base + quarter + part] = rest[from_rest]
    for i, ref in enumerate((other_0, other_1, other_2, other_3)):
        ref[...] = spare[i * ref.shape[0] : (i + 1) * ref.shape[0]]


def split_body(count, mine, *refs):
    got, keep, sends, total = refs[:count], refs[count], refs[count + 1 : -1], refs[-1]
    base = 0
    for ref in got:
        at = slice(base, base + ref.shape[0])
        total[at] = mine[at] + ref[...]
        base += ref.shape[0]
    bit = bit_of(2)
    rows = keep.shape[0]
    keep[...] = total[rows_at(bit, rows)]
    for i, send in enumerate(sends):
        part = send.shape[0]
        at = pl.ds(pl.multiple_of((1 - bit) * rows + i * part, 16), part)
        send[...] = total[at]


def rows_of(refs):
    base, places = 0, []
    for ref in refs:
        places.append(slice(base, base + ref.shape[0]))
        base += ref.shape[0]
    return places


def pair_body(count, keep, *refs):
    got, outs, total = refs[:count], refs[count:-1], refs[-1]
    for ref, at in zip(got, rows_of(got)):
        total[at] = keep[at] + ref[...]
    for ref, at in zip(outs, rows_of(outs)):
        ref[...] = total[at]


def unpair_body(count, *refs):
    own, got, (a, b, total) = refs[:count], refs[count : 2 * count], refs[2 * count :]
    for x, ref, at in zip(own, got, rows_of(own)):
        total[at] = x[...] + ref[...]
    for ref, at in zip((a, b), rows_of((a, b))):
        ref[...] = total[at]


def join_body(a, got_a, b, got_b, a_out, b_out):
    for stride, x, got, out in ((4, a, got_a, a_out), (2, b, got_b, b_out)):
        bit = bit_of(stride)
        rows = x.shape[0]
        out[rows_at(bit, rows)] = x[...]
        out[rows_at(1 - bit, rows)] = got[...]


def whole_body(a, got_a, b, got_b, out):
    rows = a.shape[0] // 2, b.shape[0] // 2
    y, z = bit_of(2), bit_of(4)

    def at(z, y, low):
        base = (z * 2 + y) * (rows[0] + rows[1]) + low * rows[0]
        return pl.ds(pl.multiple_of(base, 16), rows[low])

    for i in range(2):
        own = slice(i * rows[0], (i + 1) * rows[0])
        out[at(i, y, 0)] = a[own]
        out[at(i, 1 - y, 0)] = got_a[own]
        own = slice(i * rows[1], (i + 1) * rows[1])
        out[at(z, i, 1)] = b[own]
        out[at(1 - z, i, 1)] = got_b[own]


def swap(x, stride):
    n = lax.axis_size("tiles")
    return lax.ppermute(x, "tiles", [(t, t ^ stride) for t in range(n)])


def bf(rows, like):
    return Shape((rows, like.shape[1]), BF)


class Sum:
    def __init__(self, mine, others, sends, mids, share):
        self.mine, self.got = mine, [swap(other, 1) for other in others]
        self.rows, self.sends, self.mids = mine.shape[0], sends, mids
        self.a = int(share * self.rows / 32) * 16
        self.b = self.rows // 2 - self.a

    def step(self, body, rows, args, after, carry=(), scratch=()):
        outs = [bf(r, self.mine) for r in rows]
        made = call(body, outs, args, after, carry, scratch=scratch)
        return made[: len(rows)], made[len(rows) :]

    def split(self, after, carry=()):
        half = self.rows // 2
        (keep, *sends), carry = self.step(
            functools.partial(split_body, len(self.got)),
            [half] + [half // self.sends] * self.sends,
            (self.mine, *self.got),
            after,
            carry,
            [pltpu.VMEM(self.mine.shape, BF)],
        )
        self.parts = (keep, *[swap(send, 2) for send in sends])
        return keep, *carry

    def pair(self, after, carry=()):
        half = self.rows // 2
        m, carry = self.step(
            functools.partial(pair_body, len(self.parts) - 1),
            [half // self.mids] * self.mids,
            self.parts,
            after,
            carry,
            [pltpu.VMEM((half, self.mine.shape[1]), BF)],
        )
        token, stride = m[0], 8
        while 2 * stride < lax.axis_size("tiles"):
            m = [x + swap(x, stride) for x in m]
            stride *= 2
        self.parts = (*m, *[swap(x, stride) for x in m])
        return token, *carry

    def unpair(self, after, carry=()):
        (a, b), carry = self.step(
            functools.partial(unpair_body, self.mids),
            [self.a, self.b],
            self.parts,
            after,
            carry,
            [pltpu.VMEM((self.rows // 2, self.mine.shape[1]), BF)],
        )
        self.parts = a, swap(a, 4), b, swap(b, 2)
        return a, *carry

    def join(self, after, carry=()):
        (a, b), carry = self.step(
            join_body, [2 * self.a, 2 * self.b], self.parts, after, carry
        )
        self.parts = a, swap(a, 2), b, swap(b, 4)
        return a, *carry

    def whole(self, after, carry=()):
        (x,), carry = self.step(whole_body, [2 * self.rows], self.parts, after, carry)
        return x, *carry


def place_rows(x, half, slab, out, wide, sems):
    count = x.shape[0] // 4
    rows = wide.shape[0] // 4
    copies = []
    for i in range(4):
        at = slice(i * rows, (i + 1) * rows)
        wide[at] = x[i * count : i * count + rows].astype(F32)
        to = pl.ds(pl.multiple_of(half * 4 * rows + i * rows, rows), rows)
        copies.append(pltpu.make_async_copy(wide.at[at], out.at[slab, to], sems.at[i]))
        copies[-1].start()
    return copies


def place_body(slab, flip, *refs):
    x, out, token, wide, sems = refs[0], refs[-4], refs[-3], refs[-2], refs[-1]
    copies = place_rows(x, (bit_of(1) + flip) % 2, slab, out, wide, sems)
    token[...] = jnp.zeros(token.shape, F32)
    for copy in copies:
        copy.wait()


def place(slab, flip, x, shape, held, after):
    hid = shape.shape[1]
    return call(
        functools.partial(place_body, slab, flip),
        (shape, Shape((8, 128), F32)),
        (x,) if held is None else (x, held),
        after,
        specs=[VMEM] if held is None else [VMEM, HBM],
        out_specs=(HBM, VMEM),
        scratch=[pltpu.VMEM((hid // 2, hid), F32), pltpu.SemaphoreType.DMA((4,))],
        aliases={} if held is None else {1: 0},
    )


def finish_body(
    n, x, got, held, out, lead_out, readout_out, own_out, wide, rest, lead, turned, sems
):
    hid = out.shape[1]
    levels = lead.shape[0] // 2
    bit = bit_of(1)
    quarter, part = hid // 8, rest.shape[0] // 8
    for ref, b in ((x, bit), (got, 1 - bit)):
        for i in range(4):
            at = pl.ds(pl.multiple_of(b * 4 * part + i * part, part), part)
            base = i * (quarter + part) + quarter
            rest[at] = ref[base : base + part].astype(F32)
    a = KEPT + n
    zeros = jnp.zeros((levels - KEPT, hid), F32)
    turned[...] = jnp.concatenate([rest[a + KEPT : a + 2 * KEPT], zeros], 0).T
    copies = [pltpu.make_async_copy(turned, readout_out, sems.at[5])]
    copies[0].start()
    lead[: KEPT - 2] = rest[: KEPT - 2]
    lead[KEPT - 2 : levels] = jnp.zeros((levels - KEPT + 2, hid), F32)
    lead[levels : levels + KEPT] = rest[a : a + KEPT]
    lead[levels + KEPT :] = zeros
    copies.append(pltpu.make_async_copy(lead, lead_out, sems.at[4]))
    copies[-1].start()
    copies += place_rows(got, 1 - bit, 0, out, wide, sems)
    own_out[...] = rest[pl.ds(KEPT + lax.axis_index("tiles"), 1)]
    for copy in copies:
        copy.wait()


def local(
    warmth,
    brine,
    flags,
    tally,
    assigned,
    desired,
    intercepts,
    leading,
    interior,
    readout,
):
    n = lax.axis_size("tiles")
    lon, lat, levels = warmth.shape
    cols = lon * lat
    hid = leading.shape[1]
    scale = 1.0 / math.sqrt(cols * n)

    wide = (lon, lat, levels)
    depth = jnp.where(flags > 0, tally, 0).astype(F32)
    depth = jnp.broadcast_to(depth[:, :, None], wide)
    owner = jnp.broadcast_to(assigned[:, :, None].astype(F32), wide)
    odd = bit_of(1) == 1
    first = jnp.stack([warmth[:1], brine[:1], depth[:1]])
    last = jnp.stack([warmth[-1:], brine[-1:], depth[-1:]])
    near = swap(jnp.where(odd, first, last), 1)
    pairs = [(t, (t + 1) % n if t % 2 else (t - 1) % n) for t in range(n)]
    far = lax.ppermute(jnp.where(odd, last, first), "tiles", pairs)
    bias = lax.all_to_all(
        jnp.broadcast_to(intercepts.reshape(1, hid // 128, 128), (n, hid // 128, 128)),
        "tiles",
        split_axis=0,
        concat_axis=0,
        tiled=True,
    )
    warmth, brine, desired, leading, interior, readout = [
        pltpu.with_memory_space_constraint(a, pltpu.HBM)
        for a in (warmth, brine, desired, leading, interior, readout)
    ]
    warmth, brine, desired = call(
        stage_body,
        [pltpu.VMEM(a.shape, a.dtype) for a in (warmth, brine, desired)],
        (warmth, brine, desired),
        specs=[HBM] * 3,
        scratch=[pltpu.SemaphoreType.DMA((3,))],
    )
    stepped, pack = call(
        step_body,
        (Shape((2,) + wide, F32), Shape((cols, 2 * levels), BF)),
        (depth, near, far, owner, warmth, brine, desired),
        bias,
    )
    pack_p = swap(pack, 4)
    act = Shape((cols, hid), BF)
    one = pltpu.VMEM(act.shape, BF)
    sem = pltpu.SemaphoreType.DMA((interior.shape[0] + 2,))
    trained = (act,) * 5 + (Shape(pack.shape, BF), Shape((KEPT, hid), F32))
    scratch = [pltpu.VMEM(interior.shape, BF), pltpu.VMEM(readout.shape, BF), one, one, sem]
    inferred, w_lead, act0, act1, slope0, slope1, delta2, feat, rest = call(
        functools.partial(forward_body, n, scale),
        (Shape(wide, BF), Shape(leading.shape, BF)) + trained,
        (pack, bias, leading, interior, readout),
        specs=[VMEM] * 2 + [HBM] * 3,
        scratch=scratch,
        room=ROOM,
    )
    half = Shape((hid // 4, hid), BF)
    act0_p, act1_p, slope0_p, slope1_p, delta2_p, feat_p, rest_p, other = call(
        functools.partial(partner_body, scale),
        trained + (half,),
        (pack_p, w_lead, interior, readout, act1, delta2),
        specs=[VMEM] * 2 + [HBM] * 2 + [VMEM] * 2,
        scratch=scratch,
        room=ROOM,
    )
    mine, begun = call(
        middle_body,
        (half, Shape((cols, hid // 2), BF)),
        (interior, act1, delta2, act1_p, delta2_p, slope1),
        specs=[HBM] + [VMEM] * 5,
        scratch=[pltpu.VMEM((hid // 2, hid), BF), sem],
        room=ROOM,
    )
    top = Sum(mine, [other], 1, 1, TOP_SHARE)
    (token,) = top.split(begun)
    rows = rest_rows(n)
    part = Shape((hid // 4 + rows // 4, hid), BF)
    mine, *others = call(
        functools.partial(first_body, n),
        (part,) + (bf(part.shape[0] // 4, part),) * 4,
        (
            interior,
            feat,
            act0,
            slope0,
            slope1,
            delta2,
            begun,
            rest,
            feat_p,
            act0_p,
            slope0_p,
            slope1_p,
            delta2_p,
            rest_p,
        ),
        token,
        specs=[HBM] + [VMEM] * 13,
        scratch=[
            *[one] * 4,
            pltpu.VMEM((rows, hid), BF),
            pltpu.VMEM(part.shape, BF),
            pltpu.VMEM(interior.shape, BF),
            sem,
        ],
        room=ROOM,
    )
    low = Sum(mine, others, LOW_SENDS, LOW_MIDS, LOW_SHARE)
    (token,) = top.pair(mine)
    (token,) = low.split(token)
    (token,) = top.unpair(token)
    (token,) = low.pair(token)
    (token,) = top.join(token)
    (token,) = low.unpair(token)
    (x,) = top.whole(token)
    grads = Shape((interior.shape[0], hid, hid), F32)
    token, x = low.join(None, [x])
    held, token = place(1, 0, x, grads, None, token)
    held, token = place(1, 1, swap(x, 1), grads, held, token)
    (y,) = low.whole(token)
    held, _ = place(0, 0, y, grads, held, None)
    interior_out, lead_out, readout_out, own_out = call(
        functools.partial(finish_body, n),
        (
            grads,
            Shape((2 * levels, hid), F32),
            Shape((hid, levels), F32),
            Shape((1, hid), F32),
        ),
        (y, swap(y, 1), held),
        specs=[VMEM, VMEM, HBM],
        out_specs=(HBM, HBM, HBM, VMEM),
        scratch=[
            pltpu.VMEM((hid // 2, hid), F32),
            pltpu.VMEM((rows, hid), F32),
            pltpu.VMEM((2 * levels, hid), F32),
            pltpu.VMEM((hid, levels), F32),
            pltpu.SemaphoreType.DMA((6,)),
        ],
        aliases={2: 0},
    )
    return stepped, inferred, lead_out, interior_out, readout_out, own_out


def solution(mesh):
    part = ("groups", "tiles")
    return jax.shard_map(
        local,
        mesh=mesh,
        in_specs=(
            P(part, None, None),
            P(part, None, None),
            P(part, None),
            P(part, None),
            P(part, None),
            P(part, None, None),
            P(part, None),
            P(),
            P(),
            P(),
        ),
        out_specs=(
            P(None, part, None, None),
            P(part, None, None),
            P("groups", None),
            P(None, "groups", None),
            P("groups", None),
            P(part, None),
        ),
        check_vma=False,
    )
```

```python
import functools
import math

import jax
import jax.numpy as jnp
from jax import lax
from jax.experimental import pallas as pl
from jax.experimental.pallas import tpu as pltpu
from jax.sharding import PartitionSpec as P

KAPPA = 0.2
KEPT = 80
PACKED = 48
BLOCK = 256
ROOM = 28
TOP_SHARE = 0.625
LOW_SHARE = 0.5
LOW_SENDS = 2
LOW_MIDS = 2
BF = jnp.bfloat16
F32 = jnp.float32
VMEM = pl.BlockSpec(memory_space=pltpu.VMEM)
ANY = pl.BlockSpec(memory_space=pl.ANY)
HBM = pl.BlockSpec(memory_space=pltpu.HBM)
Shape = jax.ShapeDtypeStruct


def contract_rows(left, right):
    return lax.dot_general(left, right, (((0,), (0,)), ((), ())), preferred_element_type=F32)


def times_transposed(left, right):
    return lax.dot_general(left, right, (((1,), (1,)), ((), ())), preferred_element_type=F32)


def bit_of(stride):
    return (lax.axis_index("tiles") // stride) % 2


def rows_at(index, rows):
    return pl.ds(pl.multiple_of(index * rows, rows), rows)


def rest_rows(n):
    return -(-(n + 3 * KEPT) // 256) * 256


def call(
    body, outs, args, after=None, carry=(), specs=None, out_specs=None, scratch=(), aliases=None, room=12
):
    outs, args = tuple(outs), tuple(args)
    specs = list(specs or [VMEM] * len(args))
    out_specs = list(out_specs or [VMEM] * len(outs))
    count, made = len(args), len(outs)
    aliases = dict(aliases or {})
    extra = (() if after is None else (after,)) + tuple(carry)
    for i, array in enumerate(carry):
        aliases[count + len(extra) - len(carry) + i] = made + i
    plain = body

    def body(*refs):
        given = refs[:count]
        rest = refs[count + len(extra) :]
        plain(*given, *rest[:made], *rest[made + len(carry) :])

    return pl.pallas_call(
        body,
        out_shape=outs + tuple(Shape(a.shape, a.dtype) for a in carry),
        in_specs=specs + [ANY] * len(extra),
        out_specs=tuple(out_specs + [ANY] * len(carry)),
        scratch_shapes=scratch,
        input_output_aliases=aliases,
        compiler_params=pltpu.CompilerParams(vmem_limit_bytes=room * 2**20),
        cost_estimate=pl.CostEstimate(flops=1, bytes_accessed=1, transcendentals=0),
    )(*args, *extra)


def activate(v):
    s = 0.5 + 0.5 * jnp.tanh(0.5 * v)
    act = (v * s).astype(BF)
    s = s.astype(BF)
    return act, s + act * (1.0 - s)


def stage_body(*refs):
    count = len(refs) // 2
    copies = [
        pltpu.make_async_copy(refs[i], refs[count + i], refs[-1].at[i]) for i in range(count)
    ]
    for copy in copies:
        copy.start()
    for copy in copies:
        copy.wait()


def step_body(planes, near, far, warm, brine, desired, stepped, pack):
    lon, lat, levels = warm.shape
    cols = lon * lat
    odd = bit_of(1) == 1
    before = jnp.where(odd, near[...], far[...])
    after = jnp.where(odd, far[...], near[...])
    level = lax.broadcasted_iota(jnp.int32, (lon, lat, levels), 2).astype(F32)
    row = lax.broadcasted_iota(jnp.int32, (lon, lat, levels), 1)
    wet = (level < planes[0]).astype(F32)
    wet_b = (level[:1] < before[2]).astype(F32)
    wet_a = (level[:1] < after[2]).astype(F32)
    wet_e = jnp.concatenate([wet[1:], wet_a], 0)
    wet_w = jnp.concatenate([wet_b, wet[:-1]], 0)
    wet_n = jnp.where(row < lat - 1, pltpu.roll(wet, lat - 1, 1), 0.0)
    wet_s = jnp.where(row > 0, pltpu.roll(wet, 1, 1), 0.0)
    lane = lax.broadcasted_iota(jnp.int32, (cols, levels), 1)
    target = desired[...].reshape(cols, levels).astype(F32)
    for i, ref in enumerate((warm, brine)):
        q = ref[...]
        total = wet_e * (jnp.concatenate([q[1:], after[i]], 0) - q)
        total = total + wet_w * (jnp.concatenate([before[i], q[:-1]], 0) - q)
        total = total + wet_n * (pltpu.roll(q, lat - 1, 1) - q)
        total = total + wet_s * (pltpu.roll(q, 1, 1) - q)
        out = q + KAPPA * wet * total
        stepped[i] = out
        group = (out * wet).reshape(cols, levels)
        if i == 0:
            group = jnp.where(lane == KEPT - 2, planes[1].reshape(cols, levels), group)
            group = jnp.where(lane == KEPT - 1, planes[0].reshape(cols, levels), group)
        beside = pltpu.roll(target, (KEPT - i * PACKED) % levels, 1)
        group = jnp.where(lane >= KEPT, beside, group)
        pack[:, i * levels : (i + 1) * levels] = group.astype(BF)


def weight_grad(pairs, at):
    total = None
    for act, delta in pairs:
        term = contract_rows(act[:, at], delta[...])
        total = term if total is None else total + term
    return total.astype(BF)


def back_through(delta, weights, slope, out, start=0, stop=None):
    for j in range(start, stop or out.shape[1], BLOCK):
        back = times_transposed(delta, weights[j : j + BLOCK])
        out[:, j : j + BLOCK] = (back * slope[:, j : j + BLOCK].astype(F32)).astype(BF)


def train(scale, pack, interior, readout, inferred, outs, scratch, weights):
    act0, act1, slope0, slope1, delta2, feat, rest = outs
    w_int, w_out, act2, slope2, sems = scratch
    cols = pack.shape[0]
    levels = pack.shape[1] // 2
    hid = readout.shape[0]
    deep = interior.shape[0]
    start_weights, w_lead = weights
    start_weights()
    copies = [
        pltpu.make_async_copy(interior.at[i], w_int.at[i], sems.at[i]) for i in range(deep)
    ]
    copies.append(pltpu.make_async_copy(readout, w_out, sems.at[deep]))
    for copy in copies:
        copy.start()
    groups = [pack[:, i * levels : (i + 1) * levels].astype(F32) for i in range(2)]
    lane = lax.broadcasted_iota(jnp.int32, (cols, levels), 1)
    own = lane.astype(F32) == groups[0][:, KEPT - 2 : KEPT - 1] + KEPT
    wet = lane.astype(F32) < groups[0][:, KEPT - 1 : KEPT]
    target = jnp.where(
        lane < PACKED,
        pltpu.roll(groups[0], levels - KEPT, 1),
        pltpu.roll(groups[1], levels - KEPT + PACKED, 1),
    )
    for i, group in enumerate(groups):
        hot = jnp.where(own, 1.0, 0.0)
        feat[:, i * levels : (i + 1) * levels] = jnp.where(lane < KEPT - 2, group, hot).astype(BF)
    w_lead = w_lead()
    for layer, (left, right, act, slope) in enumerate(
        (
            (feat, w_lead, act0, slope0),
            (act0, w_int.at[0], act1, slope1),
            (act1, w_int.at[1], act2, slope2),
        )
    ):
        if layer:
            copies[layer - 1].wait()
        for j in range(0, hid, BLOCK):
            pre = jnp.dot(left[...], right[:, j : j + BLOCK], preferred_element_type=F32)
            act[:, j : j + BLOCK], slope[:, j : j + BLOCK] = activate(pre)
    copies[deep].wait()
    output = jnp.dot(act2[...], w_out[...], preferred_element_type=F32)
    if inferred is not None:
        inferred[...] = output.astype(BF).reshape(inferred.shape)
    err = jnp.where(wet, (output - target) * scale, 0.0).astype(BF)
    back_through(err, w_out, slope2, delta2)
    rest[...] = contract_rows(err, act2[...])[:KEPT]


def forward_body(n, scale, pack, bias, leading, interior, readout, *refs):
    inferred, w_lead, refs = refs[0], refs[1], refs[2:]
    copy = pltpu.make_async_copy(leading, w_lead, refs[-1].at[interior.shape[0] + 1])

    def weights():
        copy.wait()
        for j in range(bias.shape[1]):
            value = bias[:, j]
            high = value.astype(BF)
            at = slice(j * bias.shape[2], (j + 1) * bias.shape[2])
            low = (value - high.astype(F32)).astype(BF)
            w_lead[KEPT : KEPT + n, at] = high
            w_lead[bias.shape[2] + KEPT : bias.shape[2] + KEPT + n, at] = low
        return w_lead

    train(scale, pack, interior, readout, inferred, refs[:7], refs[7:], (copy.start, weights))


def partner_body(
    scale, pack, w_lead, interior, readout, act1, delta2, *refs
):
    outs, other, scratch = refs[:7], refs[7], refs[8:]
    train(
        scale, pack, interior, readout, None, outs, scratch, (lambda: None, lambda: w_lead)
    )
    rows = other.shape[0]
    at = pl.ds(pl.multiple_of((1 - bit_of(1)) * 2 * rows + bit_of(4) * rows, rows), rows)
    other[...] = weight_grad(((act1, delta2), (outs[1], outs[4])), at)


def middle_body(interior, act1, delta2, act1_p, delta2_p, slope1, mine, low, w_int, sems):
    units = low.shape[1]
    copy = pltpu.make_async_copy(interior.at[1, pl.ds(0, units)], w_int, sems.at[0])
    copy.start()
    rows = mine.shape[0]
    at = pl.ds(pl.multiple_of(bit_of(1) * 2 * rows + bit_of(4) * rows, rows), rows)
    mine[...] = weight_grad(((act1, delta2), (act1_p, delta2_p)), at)
    copy.wait()
    back_through(delta2[...], w_int, slope1, low)


def first_body(
    n,
    interior,
    feat,
    act0,
    slope0,
    slope1,
    delta2,
    low,
    rest_in,
    feat_p,
    act0_p,
    slope0_p,
    slope1_p,
    delta2_p,
    rest_p,
    mine,
    other_0,
    other_1,
    other_2,
    other_3,
    delta1,
    delta1_p,
    delta0,
    delta0_p,
    rest,
    spare,
    w_int,
    sems,
):
    levels = feat.shape[1] // 2
    hid = slope0.shape[1]
    copies = [
        pltpu.make_async_copy(interior.at[i], w_int.at[i], sems.at[i])
        for i in range(interior.shape[0])
    ]
    for copy in reversed(copies):
        copy.start()
    units = low.shape[1]
    delta1[:, :units] = low[...]
    copies[1].wait()
    back_through(delta2[...], w_int.at[1], slope1, delta1, units)
    back_through(delta2_p[...], w_int.at[1], slope1_p, delta1_p)
    copies[0].wait()
    back_through(delta1[...], w_int.at[0], slope0, delta0)
    back_through(delta1_p[...], w_int.at[0], slope0_p, delta0_p)
    total = contract_rows(feat[...], delta0[...]) + contract_rows(feat_p[...], delta0_p[...])
    lead = total.astype(BF)
    a = KEPT + n
    rest[:a] = lead[:a]
    rest[a : a + KEPT] = lead[levels : levels + KEPT]
    rest[a + KEPT : a + 2 * KEPT] = (rest_in[...] + rest_p[...]).astype(BF)
    rows = rest.shape[0]
    if rows > a + 2 * KEPT:
        rest[a + 2 * KEPT :] = jnp.zeros((rows - a - 2 * KEPT, hid), BF)
    bit, z = bit_of(1), bit_of(4)
    quarter, part = hid // 8, rows // 8
    for ref, b in ((spare, 1 - bit), (mine, bit)):
        at = pl.ds(pl.multiple_of((b * 2 + z) * 2 * quarter, 2 * quarter), 2 * quarter)
        got = weight_grad(((act0, delta1), (act0_p, delta1_p)), at)
        for y in range(2):
            base = y * (quarter + part)
            ref[base : base + quarter] = got[y * quarter : (y + 1) * quarter]
            from_rest = pl.ds(pl.multiple_of((b * 2 + z) * 2 * part + y * part, part), part)
            ref[base + quarter : base + quarter + part] = rest[from_rest]
    for i, ref in enumerate((other_0, other_1, other_2, other_3)):
        ref[...] = spare[i * ref.shape[0] : (i + 1) * ref.shape[0]]


def split_body(count, mine, *refs):
    got, keep, sends, total = refs[:count], refs[count], refs[count + 1 : -1], refs[-1]
    base = 0
    for ref in got:
        at = slice(base, base + ref.shape[0])
        total[at] = mine[at] + ref[...]
        base += ref.shape[0]
    bit = bit_of(2)
    rows = keep.shape[0]
    keep[...] = total[rows_at(bit, rows)]
    for i, send in enumerate(sends):
        part = send.shape[0]
        at = pl.ds(pl.multiple_of((1 - bit) * rows + i * part, 16), part)
        send[...] = total[at]


def rows_of(refs):
    base, places = 0, []
    for ref in refs:
        places.append(slice(base, base + ref.shape[0]))
        base += ref.shape[0]
    return places


def pair_body(count, keep, *refs):
    got, outs, total = refs[:count], refs[count:-1], refs[-1]
    for ref, at in zip(got, rows_of(got)):
        total[at] = keep[at] + ref[...]
    for ref, at in zip(outs, rows_of(outs)):
        ref[...] = total[at]


def unpair_body(count, *refs):
    own, got, (a, b, total) = refs[:count], refs[count : 2 * count], refs[2 * count :]
    for x, ref, at in zip(own, got, rows_of(own)):
        total[at] = x[...] + ref[...]
    for ref, at in zip((a, b), rows_of((a, b))):
        ref[...] = total[at]


def join_body(a, got_a, b, got_b, a_out, b_out):
    for stride, x, got, out in ((4, a, got_a, a_out), (2, b, got_b, b_out)):
        bit = bit_of(stride)
        rows = x.shape[0]
        out[rows_at(bit, rows)] = x[...]
        out[rows_at(1 - bit, rows)] = got[...]


def whole_body(a, got_a, b, got_b, out):
    rows = a.shape[0] // 2, b.shape[0] // 2
    y, z = bit_of(2), bit_of(4)

    def at(z, y, low):
        base = (z * 2 + y) * (rows[0] + rows[1]) + low * rows[0]
        return pl.ds(pl.multiple_of(base, 16), rows[low])

    for i in range(2):
        own = slice(i * rows[0], (i + 1) * rows[0])
        out[at(i, y, 0)] = a[own]
        out[at(i, 1 - y, 0)] = got_a[own]
        own = slice(i * rows[1], (i + 1) * rows[1])
        out[at(z, i, 1)] = b[own]
        out[at(1 - z, i, 1)] = got_b[own]


def swap(x, stride):
    n = lax.axis_size("tiles")
    return lax.ppermute(x, "tiles", [(t, t ^ stride) for t in range(n)])


def bf(rows, like):
    return Shape((rows, like.shape[1]), BF)


class Sum:
    def __init__(self, mine, others, sends, mids, share):
        self.mine, self.got = mine, [swap(other, 1) for other in others]
        self.rows, self.sends, self.mids = mine.shape[0], sends, mids
        self.a = int(share * self.rows / 32) * 16
        self.b = self.rows // 2 - self.a

    def step(self, body, rows, args, after, carry=(), scratch=()):
        outs = [bf(r, self.mine) for r in rows]
        made = call(body, outs, args, after, carry, scratch=scratch)
        return made[: len(rows)], made[len(rows) :]

    def split(self, after, carry=()):
        half = self.rows // 2
        (keep, *sends), carry = self.step(
            functools.partial(split_body, len(self.got)),
            [half] + [half // self.sends] * self.sends,
            (self.mine, *self.got),
            after,
            carry,
            [pltpu.VMEM(self.mine.shape, BF)],
        )
        self.parts = (keep, *[swap(send, 2) for send in sends])
        return keep, *carry

    def pair(self, after, carry=()):
        half = self.rows // 2
        m, carry = self.step(
            functools.partial(pair_body, len(self.parts) - 1),
            [half // self.mids] * self.mids,
            self.parts,
            after,
            carry,
            [pltpu.VMEM((half, self.mine.shape[1]), BF)],
        )
        token, stride = m[0], 8
        while 2 * stride < lax.axis_size("tiles"):
            m = [x + swap(x, stride) for x in m]
            stride *= 2
        self.parts = (*m, *[swap(x, stride) for x in m])
        return token, *carry

    def unpair(self, after, carry=()):
        (a, b), carry = self.step(
            functools.partial(unpair_body, self.mids),
            [self.a, self.b],
            self.parts,
            after,
            carry,
            [pltpu.VMEM((self.rows // 2, self.mine.shape[1]), BF)],
        )
        self.parts = a, swap(a, 4), b, swap(b, 2)
        return a, *carry

    def join(self, after, carry=()):
        (a, b), carry = self.step(
            join_body, [2 * self.a, 2 * self.b], self.parts, after, carry
        )
        self.parts = a, swap(a, 2), b, swap(b, 4)
        return a, *carry

    def whole(self, after, carry=()):
        (x,), carry = self.step(whole_body, [2 * self.rows], self.parts, after, carry)
        return x, *carry


def place_rows(x, half, slab, out, wide, sems):
    count = x.shape[0] // 4
    rows = wide.shape[0] // 4
    copies = []
    for i in range(4):
        at = slice(i * rows, (i + 1) * rows)
        wide[at] = x[i * count : i * count + rows].astype(F32)
        to = pl.ds(pl.multiple_of(half * 4 * rows + i * rows, rows), rows)
        copies.append(pltpu.make_async_copy(wide.at[at], out.at[slab, to], sems.at[i]))
        copies[-1].start()
    return copies


def place_body(slab, flip, *refs):
    x, out, token, wide, sems = refs[0], refs[-4], refs[-3], refs[-2], refs[-1]
    copies = place_rows(x, (bit_of(1) + flip) % 2, slab, out, wide, sems)
    token[...] = jnp.zeros(token.shape, F32)
    for copy in copies:
        copy.wait()


def place(slab, flip, x, shape, held, after):
    hid = shape.shape[1]
    return call(
        functools.partial(place_body, slab, flip),
        (shape, Shape((8, 128), F32)),
        (x,) if held is None else (x, held),
        after,
        specs=[VMEM] if held is None else [VMEM, HBM],
        out_specs=(HBM, VMEM),
        scratch=[pltpu.VMEM((hid // 2, hid), F32), pltpu.SemaphoreType.DMA((4,))],
        aliases={} if held is None else {1: 0},
    )


def finish_body(
    n, x, got, held, out, lead_out, readout_out, own_out, wide, rest, lead, turned, sems
):
    hid = out.shape[1]
    levels = lead.shape[0] // 2
    bit = bit_of(1)
    quarter, part = hid // 8, rest.shape[0] // 8
    for ref, b in ((x, bit), (got, 1 - bit)):
        for i in range(4):
            at = pl.ds(pl.multiple_of(b * 4 * part + i * part, part), part)
            base = i * (quarter + part) + quarter
            rest[at] = ref[base : base + part].astype(F32)
    a = KEPT + n
    zeros = jnp.zeros((levels - KEPT, hid), F32)
    turned[...] = jnp.concatenate([rest[a + KEPT : a + 2 * KEPT], zeros], 0).T
    copies = [pltpu.make_async_copy(turned, readout_out, sems.at[5])]
    copies[0].start()
    lead[: KEPT - 2] = rest[: KEPT - 2]
    lead[KEPT - 2 : levels] = jnp.zeros((levels - KEPT + 2, hid), F32)
    lead[levels : levels + KEPT] = rest[a : a + KEPT]
    lead[levels + KEPT :] = zeros
    copies.append(pltpu.make_async_copy(lead, lead_out, sems.at[4]))
    copies[-1].start()
    copies += place_rows(got, 1 - bit, 0, out, wide, sems)
    own_out[...] = rest[pl.ds(KEPT + lax.axis_index("tiles"), 1)]
    for copy in copies:
        copy.wait()


def local(
    warmth,
    brine,
    flags,
    tally,
    assigned,
    desired,
    intercepts,
    leading,
    interior,
    readout,
):
    n = lax.axis_size("tiles")
    lon, lat, levels = warmth.shape
    cols = lon * lat
    hid = leading.shape[1]
    scale = 1.0 / math.sqrt(cols * n)

    wide = (lon, lat, levels)
    numbers = jnp.stack([jnp.where(flags > 0, tally, 0), assigned]).astype(F32)
    planes = jnp.broadcast_to(numbers[..., None], (2,) + wide)
    depth = planes[0]
    odd = bit_of(1) == 1
    first = jnp.stack([warmth[:1], brine[:1], depth[:1]])
    last = jnp.stack([warmth[-1:], brine[-1:], depth[-1:]])
    near = swap(jnp.where(odd, first, last), 1)
    pairs = [(t, (t + 1) % n if t % 2 else (t - 1) % n) for t in range(n)]
    far = lax.ppermute(jnp.where(odd, last, first), "tiles", pairs)
    bias = lax.all_to_all(
        jnp.broadcast_to(intercepts.reshape(1, hid // 128, 128), (n, hid // 128, 128)),
        "tiles",
        split_axis=0,
        concat_axis=0,
        tiled=True,
    )
    warmth, brine, desired, leading, interior, readout = [
        pltpu.with_memory_space_constraint(a, pltpu.HBM)
        for a in (warmth, brine, desired, leading, interior, readout)
    ]
    warmth, brine, desired = call(
        stage_body,
        [pltpu.VMEM(a.shape, a.dtype) for a in (warmth, brine, desired)],
        (warmth, brine, desired),
        specs=[HBM] * 3,
        scratch=[pltpu.SemaphoreType.DMA((3,))],
    )
    stepped, pack = call(
        step_body,
        (Shape((2,) + wide, F32), Shape((cols, 2 * levels), BF)),
        (planes, near, far, warmth, brine, desired),
        bias,
    )
    pack_p = swap(pack, 4)
    act = Shape((cols, hid), BF)
    one = pltpu.VMEM(act.shape, BF)
    sem = pltpu.SemaphoreType.DMA((interior.shape[0] + 2,))
    trained = (act,) * 5 + (Shape(pack.shape, BF), Shape((KEPT, hid), F32))
    scratch = [pltpu.VMEM(interior.shape, BF), pltpu.VMEM(readout.shape, BF), one, one, sem]
    inferred, w_lead, act0, act1, slope0, slope1, delta2, feat, rest = call(
        functools.partial(forward_body, n, scale),
        (Shape(wide, BF), Shape(leading.shape, BF)) + trained,
        (pack, bias, leading, interior, readout),
        specs=[VMEM] * 2 + [HBM] * 3,
        scratch=scratch,
        room=ROOM,
    )
    half = Shape((hid // 4, hid), BF)
    act0_p, act1_p, slope0_p, slope1_p, delta2_p, feat_p, rest_p, other = call(
        functools.partial(partner_body, scale),
        trained + (half,),
        (pack_p, w_lead, interior, readout, act1, delta2),
        specs=[VMEM] * 2 + [HBM] * 2 + [VMEM] * 2,
        scratch=scratch,
        room=ROOM,
    )
    mine, begun = call(
        middle_body,
        (half, Shape((cols, hid // 2), BF)),
        (interior, act1, delta2, act1_p, delta2_p, slope1),
        specs=[HBM] + [VMEM] * 5,
        scratch=[pltpu.VMEM((hid // 2, hid), BF), sem],
        room=ROOM,
    )
    top = Sum(mine, [other], 1, 1, TOP_SHARE)
    (token,) = top.split(begun)
    rows = rest_rows(n)
    part = Shape((hid // 4 + rows // 4, hid), BF)
    mine, *others = call(
        functools.partial(first_body, n),
        (part,) + (bf(part.shape[0] // 4, part),) * 4,
        (
            interior,
            feat,
            act0,
            slope0,
            slope1,
            delta2,
            begun,
            rest,
            feat_p,
            act0_p,
            slope0_p,
            slope1_p,
            delta2_p,
            rest_p,
        ),
        token,
        specs=[HBM] + [VMEM] * 13,
        scratch=[
            *[one] * 4,
            pltpu.VMEM((rows, hid), BF),
            pltpu.VMEM(part.shape, BF),
            pltpu.VMEM(interior.shape, BF),
            sem,
        ],
        room=ROOM,
    )
    low = Sum(mine, others, LOW_SENDS, LOW_MIDS, LOW_SHARE)
    (token,) = top.pair(mine)
    (token,) = low.split(token)
    (token,) = top.unpair(token)
    (token,) = low.pair(token)
    (token,) = top.join(token)
    (token,) = low.unpair(token)
    (x,) = top.whole(token)
    grads = Shape((interior.shape[0], hid, hid), F32)
    token, x = low.join(None, [x])
    held, token = place(1, 0, x, grads, None, token)
    held, token = place(1, 1, swap(x, 1), grads, held, token)
    (y,) = low.whole(token)
    held, _ = place(0, 0, y, grads, held, None)
    interior_out, lead_out, readout_out, own_out = call(
        functools.partial(finish_body, n),
        (
            grads,
            Shape((2 * levels, hid), F32),
            Shape((hid, levels), F32),
            Shape((1, hid), F32),
        ),
        (y, swap(y, 1), held),
        specs=[VMEM, VMEM, HBM],
        out_specs=(HBM, HBM, HBM, VMEM),
        scratch=[
            pltpu.VMEM((hid // 2, hid), F32),
            pltpu.VMEM((rows, hid), F32),
            pltpu.VMEM((2 * levels, hid), F32),
            pltpu.VMEM((hid, levels), F32),
            pltpu.SemaphoreType.DMA((6,)),
        ],
        aliases={2: 0},
    )
    return stepped, inferred, lead_out, interior_out, readout_out, own_out


def solution(mesh):
    part = ("groups", "tiles")
    return jax.shard_map(
        local,
        mesh=mesh,
        in_specs=(
            P(part, None, None),
            P(part, None, None),
            P(part, None),
            P(part, None),
            P(part, None),
            P(part, None, None),
            P(part, None),
            P(),
            P(),
            P(),
        ),
        out_specs=(
            P(None, part, None, None),
            P(part, None, None),
            P("groups", None),
            P(None, "groups", None),
            P("groups", None),
            P(part, None),
        ),
        check_vma=False,
    )
```
